512 devices in a mesh: row: 32 (over x_hi, y, core), col: 16 (over z, x_lo).
Axes of the slice: x: 4 (x_hi: 2, x_lo: 2; x = x_hi * 2 + x_lo), y: 8, z: 8, core: 2. Of those that a mesh axis runs over, the one named last changes fastest.
Arguments:
- timelines: bfloat16 [16384, 1024], P(('row', 'col')), may hold values from -0.3984375 to 0.3984375
- windows: bfloat16 [512, 16, 1024], P('row', 'col'), may hold values from -0.3984375 to 0.3984375
- row_gap: int32 [16384], P(('row', 'col')), may hold values from 0 to 11
- col_gap: int32 [512, 16], P('row', 'col'), may hold values from 0 to 11
- positive: int32 [16384], P(('row', 'col')), may hold values from 0 to 8191
- natural_exponent_factor: float32 [1], replicated, may hold values from 1.6 to 2.4
- bias: float32 [1], replicated, may hold values from -5 to -3
- bucket_deduction: float32 [8], replicated, may hold values from 0.1 to 3
Outputs:
- mean_loss: float32 [1], replicated
- grad_timelines: float32 [16384, 1024], P(('row', 'col'))
- grad_windows: float32 [512, 16, 1024], P('row', 'col')
- mean_grad_bias: float32 [1], replicated
- mean_grad_temp: float32 [1], replicated
- mean_grad_penalty: float32 [8], replicated
The draws below stay inside these ranges and needn't reach their ends.
All inputs are finite; a program needn't handle non-finite values.
Results may differ from the reference program's by a relative error of at most 0.0025.
Values may be sent and summed in bfloat16 or wider, within the bound.
A program may use at most 64 MiB of HBM per device.

```python
import math
import jax
import jax.numpy as jnp
from jax import lax

D = 1024
NBK = 8
CB = 512
NR = 16384
NC = 8192
N_ROW = 32
N_COL = 16


def with_ends(entries, rng, least, largest):
    place = [jax.random.randint(jax.random.fold_in(rng, axis), (), 0, length) for axis, length in enumerate(entries.shape)]
    widest = entries.shape.index(max(entries.shape))
    next_to = place[:widest] + [(place[widest] + 1) % entries.shape[widest]] + place[widest + 1:]
    return entries.at[tuple(place)].set(least).at[tuple(next_to)].set(largest)


def steps_of(stream_key, extent, pieces, smallest, largest):
    level, own = 1.0, jax.random.fold_in(stream_key, 6)
    for dim, blocks in pieces:
        steps = jnp.exp(jax.random.uniform(jax.random.fold_in(own, dim), (blocks,), jnp.float32, smallest / len(pieces), largest / len(pieces)))
        level = level * jnp.repeat(steps, extent[dim] // blocks).reshape([-1 if axis == dim else 1 for axis in range(len(extent))])
    return level


def gaussian(stream_key, dims, scale, bound, pieces=(), held_as=jnp.bfloat16):
    array = scale * jax.random.normal(stream_key, dims, jnp.float32)
    if pieces:
        array = array * steps_of(stream_key, dims, pieces, -0.22, 0.18)
    return jnp.clip(array, -bound, bound).astype(held_as)


def setup_inputs(seed: int = 0) -> dict:
    key_list = jax.random.split(jax.random.key(seed), 9)
    return {
        "timelines": gaussian(key_list[0], (NR, D), 0.06, 0.3984375, ((0, 512),)),
        "windows": gaussian(key_list[1], (CB, N_COL, D), 0.06, 0.3984375, ((0, 32), (1, 16))),
        "row_gap": with_ends(jax.random.randint(key_list[2], (NR,), 0, 12), jax.random.fold_in(key_list[2], 1), 0, 11).astype(jnp.int32),
        "col_gap": with_ends(jax.random.randint(key_list[3], (CB, N_COL), 0, 12), jax.random.fold_in(key_list[3], 1), 0, 11).astype(jnp.int32),
        "positive": with_ends(jax.random.randint(key_list[4], (NR,), 0, NC), jax.random.fold_in(key_list[4], 1), 0, NC - 1).astype(jnp.int32),
        "natural_exponent_factor": jnp.clip(jax.random.uniform(key_list[5], (1,), jnp.float32, 1.6, 2.4), 1.6, 2.4),
        "bias": jnp.clip(jax.random.uniform(key_list[6], (1,), jnp.float32, -5.0, -3.0), -5.0, -3.0),
        "bucket_deduction": jnp.clip(jnp.exp(jax.random.uniform(key_list[7], (NBK,), jnp.float32, math.log(0.1), math.log(3.0))), 0.1, 3.0),
    }


def derivative_segments(history_vector_segment, history_interval_buckets, history_match_labels, upcoming_vector_segment, upcoming_interval_buckets, target_ordinal, sharpness_factor, score_shift, bucket_deduction):
    inner_products_matrix = lax.dot_general(history_vector_segment, upcoming_vector_segment, (((1,), (1,)), ((), ())), preferred_element_type=jnp.float32)
    gap_bucket = jnp.minimum(jnp.abs(history_interval_buckets[:, None] - upcoming_interval_buckets[None, :]), bucket_deduction.shape[0] - 1)
    attenuated_scores = jnp.zeros(inner_products_matrix.shape, jnp.float32)
    for bucket in range(bucket_deduction.shape[0]):
        attenuated_scores = jnp.where(gap_bucket == bucket, bucket_deduction[bucket], attenuated_scores)
    match_scores = sharpness_factor * inner_products_matrix + score_shift - attenuated_scores
    labels = jnp.where(history_match_labels[:, None] == target_ordinal[None, :], jnp.float32(1.0), jnp.float32(-1.0))
    match_objective = jnp.sum(jax.nn.softplus(-labels * match_scores))
    objective_derivative = -labels * jax.nn.sigmoid(-labels * match_scores)
    derivative_narrowed = objective_derivative.astype(jnp.bfloat16)
    deduction_derivative = jnp.stack([-jnp.sum(jnp.where(gap_bucket == bucket, objective_derivative, jnp.float32(0.0))) for bucket in range(bucket_deduction.shape[0])])
    objective_tallies = (match_objective, jnp.sum(objective_derivative), jnp.sum(objective_derivative * inner_products_matrix) * sharpness_factor, deduction_derivative)
    return derivative_narrowed, objective_tallies


def reference(timelines, windows, row_gap, col_gap, positive, natural_exponent_factor, bias, bucket_deduction):
    block_cols = windows.shape[0]
    col_count = windows.shape[1]
    width = windows.shape[2]
    total_rows = timelines.shape[0]
    total_cols = block_cols * col_count
    collected_target_vectors = jnp.transpose(windows, (1, 0, 2)).reshape(total_cols, width)
    collected_interval_buckets = jnp.transpose(col_gap).reshape(total_cols)
    target_ordinal = jnp.arange(total_cols, dtype=jnp.int32)
    upcoming_joined_vectors = collected_target_vectors.reshape(col_count, block_cols, width).astype(jnp.float32)
    sharpness_factor = jnp.exp(natural_exponent_factor[0])
    score_shift = bias[0]
    blocks = N_ROW
    block_rows = total_rows // blocks
    time_blocks = timelines.reshape(blocks, block_rows, width)
    gap_blocks = row_gap.reshape(blocks, block_rows)
    pos_blocks = positive.reshape(blocks, block_rows)

    def one_block(running, inputs):
        win_sum, objective_tallies = running
        present_target_vectors, present_interval_buckets, present_match_labels = inputs
        derivative_narrowed, refreshed_tallies = derivative_segments(present_target_vectors, present_interval_buckets, present_match_labels, collected_target_vectors, collected_interval_buckets, target_ordinal, sharpness_factor, score_shift, bucket_deduction)
        derivative_averaged = derivative_narrowed.astype(jnp.float32).reshape(block_rows, col_count, block_cols)
        history_incomplete_terms = sharpness_factor * jnp.einsum("jfg,fgs->fjs", derivative_averaged, upcoming_joined_vectors)
        time_grad = jnp.sum(history_incomplete_terms, axis=0)
        upcoming_incomplete_term = sharpness_factor * lax.dot_general(derivative_narrowed, present_target_vectors, (((0,), (0,)), ((), ())), preferred_element_type=jnp.float32)
        objective_tallies = jax.tree.map(lambda old, add: old + add, objective_tallies, refreshed_tallies)
        return (win_sum + upcoming_incomplete_term, objective_tallies), time_grad

    zero_stats = (jnp.float32(0.0), jnp.float32(0.0), jnp.float32(0.0), jnp.zeros((bucket_deduction.shape[0],), jnp.float32))
    init = (jnp.zeros((total_cols, width), jnp.float32), zero_stats)
    (win_sum, objective_tallies), time_grads = lax.scan(one_block, init, (time_blocks, gap_blocks, pos_blocks))
    grad_timelines = time_grads.reshape(total_rows, width)
    grad_windows = jnp.transpose(win_sum.reshape(col_count, block_cols, width), (1, 0, 2))
    pairs = jnp.float32(total_rows) * jnp.float32(total_cols)
    mean_loss = jnp.reshape(objective_tallies[0] / pairs, (1,))
    mean_grad_bias = jnp.reshape(objective_tallies[1] / pairs, (1,))
    mean_grad_temp = jnp.reshape(objective_tallies[2] / pairs, (1,))
    mean_grad_penalty = objective_tallies[3] / pairs
    return (mean_loss, grad_timelines, grad_windows, mean_grad_bias, mean_grad_temp, mean_grad_penalty)
```

```python
import jax
import jax.numpy as jnp
from jax import lax
from jax.experimental import pallas as pl
from jax.experimental.pallas import tpu as pltpu
from jax.sharding import PartitionSpec as P

MESH = pl.DeviceIdType.MESH
F32 = jnp.float32
BF16 = jnp.bfloat16

D = 1024
DE = D + 128
XR = 32
YR = 16
NZ, NY, NX = 8, 8, 4
NR = XR * NZ * 2
NW = YR * NY * NX
HALF = NR // 2
PAIRS = 134217728
SIZES = {"core": 2, "x": NX, "y": NY, "z": NZ}
GROUP = (
    [{"z": k} for k in range(1, NZ)]
    + [{"y": k} for k in range(1, NY)]
    + [{"x": k} for k in range(1, NX)]
    + [{"core": 1}]
)
NT = (((1,), (1,)), ((), ()))
TN = (((0,), (0,)), ((), ()))


def position():
    row, col = lax.axis_index("row"), lax.axis_index("col")
    return {
        "core": row % 2,
        "y": (row // 2) % NY,
        "x": (row // (2 * NY)) * 2 + col % 2,
        "z": col // 2,
    }


def device(me, off):
    at = dict(me)
    for axis, k in off.items():
        at[axis] = (me[axis] + (k + SIZES[axis])) % SIZES[axis]
    return ((at["x"] // 2) * (2 * NY) + at["y"] * 2 + at["core"], at["z"] * 2 + at["x"] % 2)


def rows(start, count):
    return pl.ds(start, count)


def dot(a, b, dims):
    return lax.dot_general(a, b, dims, preferred_element_type=F32)


def kernel(
    nef_ref, bias_ref, ded_ref, t_ref, w_ref, gap_ref, pos_ref, colgap_ref,
    gt_ref, gw_ref, stat_ref,
    xg, yg, oh, pt, sim, dm, slope, slope_lo,
    dx, dx_core, dx_send, dx_far, dx_half, dx_near, dx_mid, dx_next,
    dy, dy_send, dy_x2, dy_x1, dy_sum, dy_far, dy_half, dy_mid, dy_near, dy_next,
    st_core, st_z, st_y, st_x,
    send_sem, recv_sem,
):
    me = position()
    barrier = pltpu.get_barrier_semaphore()
    for off in GROUP:
        pl.semaphore_signal(barrier, inc=1, device_id=device(me, off), device_id_type=MESH)

    started = []

    def send(src, dst, off):
        i = len(started)
        copy = pltpu.make_async_remote_copy(
            src_ref=src,
            dst_ref=dst,
            send_sem=send_sem.at[i],
            recv_sem=recv_sem.at[i],
            device_id=device(me, off),
            device_id_type=MESH,
        )
        copy.start()
        started.append(copy)
        return copy

    lane = lax.broadcasted_iota(jnp.int32, (XR, 128), 1)
    diagonal = lax.broadcasted_iota(jnp.int32, (XR, XR), 0) == lax.broadcasted_iota(
        jnp.int32, (XR, XR), 1
    )

    def column(ref):
        row = jnp.broadcast_to(ref[...].astype(F32), (XR, XR))
        return jnp.sum(jnp.where(diagonal, row, 0.0), axis=1, keepdims=True)

    gap, pos = column(gap_ref), column(pos_ref)
    pos_high = jnp.floor(pos * (1.0 / 128.0))
    pos_low = pos - 128.0 * pos_high
    extra = jnp.where(
        lane == 0, gap, jnp.where(lane == 1, pos_high, jnp.where(lane == 2, pos_low, 0.0))
    )
    xg[0:XR, 0:D] = t_ref[...]
    xg[0:XR, D:DE] = extra.astype(BF16)
    yg[0:YR, 0:D] = w_ref[...]
    yg[0:YR, D:DE] = jnp.broadcast_to(colgap_ref[...].astype(F32), (YR, 128)).astype(BF16)

    pl.semaphore_wait(barrier, len(GROUP))

    def xs(k):
        return xg.at[pl.ds((k % NZ) * XR, XR)]

    def xs_other(k):
        return xg.at[pl.ds(HALF + (k % NZ) * XR, XR)]

    def ys(i, j):
        return yg.at[pl.ds(((i % NX) * NY + j % NY) * YR, YR)]

    lo_cols, hi_cols = pl.ds(0, 512), pl.ds(512, DE - 512)

    zp2 = send(xs(0), xs(-2), {"z": 2})
    zm2 = send(xs(0), xs(2), {"z": -2})
    yp2 = send(ys(0, 0), ys(0, -2), {"y": 2})
    ym2 = send(ys(0, 0), ys(0, 2), {"y": -2})
    xp = {0: send(ys(0, 0), ys(-1, 0), {"x": 1})}
    xm = {0: send(ys(0, 0), ys(1, 0), {"x": -1})}
    yp1 = send(ys(0, 0), ys(0, -1), {"y": 1})
    ym1 = send(ys(0, 0), ys(0, 1), {"y": -1})
    zp1 = send(xs(0), xs(-1), {"z": 1})
    zm1 = send(xs(0), xs(1), {"z": -1})
    core = {0: send(xs(0), xs_other(0), {"core": 1})}

    def to_x(j):
        xp[j] = send(ys(0, j), ys(-1, j), {"x": 1})
        xm[j] = send(ys(0, j), ys(1, j), {"x": -1})

    def to_core(k):
        core[k] = send(xs(k), xs_other(k), {"core": 1})

    zp2.wait_recv()
    zp3 = send(xs(-2), xs(-3), {"z": 1})
    zp4 = send(xs(-2).at[pl.ds(0, 16)], xs(4).at[pl.ds(0, 16)], {"z": 2})
    zm2.wait_recv()
    zm3 = send(xs(2), xs(3), {"z": -1})
    zm4 = send(xs(2).at[pl.ds(16, 16)], xs(4).at[pl.ds(16, 16)], {"z": -2})
    yp2.wait_recv()
    yp3 = send(ys(0, -2), ys(0, -3), {"y": 1})
    yp4 = send(ys(0, -2).at[:, lo_cols], ys(0, 4).at[:, lo_cols], {"y": 2})
    to_x(-2)
    ym2.wait_recv()
    ym3 = send(ys(0, 2), ys(0, 3), {"y": -1})
    ym4 = send(ys(0, 2).at[:, hi_cols], ys(0, 4).at[:, hi_cols], {"y": -2})
    to_x(2)
    yp1.wait_recv()
    to_x(-1)
    ym1.wait_recv()
    to_x(1)
    zp1.wait_recv()
    to_core(-1)
    zm1.wait_recv()
    to_core(1)
    to_core(-2)
    to_core(2)
    by_plus, by_minus = (0, -2, -1, -3), (2, 1, 3, 4)
    far = []

    def onward(j):
        if j in by_plus:
            xp[j].wait_recv()
            far.append(send(ys(-1, j), ys(2, j), {"x": 1}))
        else:
            xm[j].wait_recv()
            far.append(send(ys(1, j), ys(2, j), {"x": -1}))

    onward(0)
    yp3.wait_recv()
    to_x(-3)
    ym3.wait_recv()
    to_x(3)
    yp4.wait_recv()
    ym4.wait_recv()
    to_x(4)
    zp3.wait_recv()
    to_core(-3)
    zm3.wait_recv()
    to_core(3)
    zp4.wait_recv()
    zm4.wait_recv()
    to_core(4)
    for j in (-2, 2, -1, 1, -3, 3, 4):
        onward(j)
    for j in (0, -2, 2, -1, 1, -3, 3, 4):
        (xm if j in by_plus else xp)[j].wait_recv()
    for copy in far:
        copy.wait_recv()
    for copy in core.values():
        copy.wait_recv()

    lane = lax.broadcasted_iota(jnp.int32, (64, 128), 1)
    lane16 = (lane % 16).astype(F32)
    bias = bias_ref[0]

    def tables(b, _):
        at = pl.ds(pl.multiple_of(b * 64, 64), 64)
        mine = xg[at, D:DE].astype(F32)[:, 0:1]
        oh[at, :] = jnp.where((lane16 == mine) & (lane < 48), 1.0, 0.0).astype(BF16)
        apart = jnp.abs(lane16 - yg[at, D:DE].astype(F32))
        table = jnp.full((64, 128), ded_ref[7], F32)
        for k in range(7):
            table = jnp.where(apart == float(k), ded_ref[k], table)
        table = table - bias
        first = table.astype(BF16)
        rest = table - first.astype(F32)
        second = rest.astype(BF16)
        third = (rest - second.astype(F32)).astype(BF16)
        pt[at, :] = jnp.where(
            lane < 16,
            first.astype(F32),
            jnp.where(lane < 32, second.astype(F32), jnp.where(lane < 48, third.astype(F32), 0.0)),
        ).astype(BF16)
        return 0

    lax.fori_loop(0, NR // 64, tables, 0)

    def products(b, _):
        at = pl.ds(pl.multiple_of(b * 256, 256), 256)
        sim[at, :] = dot(xg[at, 0:D], yg[:, 0:D], NT)
        dm[at, :] = dot(oh[at, :], pt[...], NT)
        return 0

    lax.fori_loop(0, NR // 256, products, 0)

    scale = jnp.exp(jnp.full((16, NW), nef_ref[0], F32))
    at_lane = lax.broadcasted_iota(jnp.int32, (1, NW), 1)
    slot = at_lane // YR
    win_y = (slot % NY + me["y"]) % NY
    win_x = (slot // NY + me["x"]) % NX
    win_row = (win_x // 2) * (2 * NY) + win_y * 2 + me["core"]
    ordinal = (me["z"] * 2 + win_x % 2) * 512 + win_row * YR + at_lane % YR
    ordinal = ordinal.astype(F32)

    def slopes(b, sums):
        at = pl.ds(pl.multiple_of(b * 16, 16), 16)
        loss_sum, temp_sum = sums
        s = scale * sim[at, :]
        logit = s - dm[at, :]
        mine = xg[at, D:DE].astype(F32)
        match = (mine[:, 1:2] * 128.0 + mine[:, 2:3]) == ordinal
        z = jnp.where(match, -logit, logit)
        e = jnp.exp(-jnp.abs(z))
        r = 1.0 / (1.0 + e)
        sig = jnp.where(z >= 0.0, r, e * r)
        grad = jnp.where(match, -sig, sig)
        loss_sum = loss_sum + (jnp.maximum(z, 0.0) + jnp.log1p(e))
        temp_sum = temp_sum + grad * s
        high = grad.astype(BF16)
        slope[at, :] = high
        slope_lo[at, :] = (grad - high.astype(F32)).astype(BF16)
        return loss_sum, temp_sum

    zero = jnp.zeros((16, NW), F32)
    loss_sum, temp_sum = lax.fori_loop(0, NR // 16, slopes, (zero, zero))

    def win_grad(b, _):
        at = pl.ds(pl.multiple_of(b * 256, 256), 256)
        dy[:, at] = dot(slope[...], xg[:, at], TN)
        return 0

    lax.fori_loop(0, D // 256, win_grad, 0)
    dy_send[0:128, :] = dy[256:384, :].astype(BF16)
    x2p = send(dy_send.at[pl.ds(0, 64)], dy_x2.at[pl.ds(0, 64)], {"x": 1})
    x2m = send(dy_send.at[pl.ds(64, 64)], dy_x2.at[pl.ds(64, 64)], {"x": -1})

    def time_grad(b, _):
        at = pl.ds(pl.multiple_of(b * 256, 256), 256)
        dx[:, at] = dot(slope[...], yg[:, at], (((1,), (0,)), ((), ())))
        return 0

    lax.fori_loop(0, D // 256, time_grad, 0)
    dx_swap = send(dx.at[pl.ds(HALF, HALF)], dx_core, {"core": 1})

    by_gap = dot(slope[...], oh[...], TN) + dot(slope_lo[...], oh[...], TN)
    lane_w = lax.broadcasted_iota(jnp.int32, (NW, 128), 1)
    apart = jnp.abs((lane_w % 16).astype(F32) - yg[:, D:DE].astype(F32))
    apart = jnp.where(lane_w < 16, jnp.minimum(apart, 7.0), 8.0)
    lane_s = lax.broadcasted_iota(jnp.int32, (8, 128), 1)

    def total(values):
        return jnp.sum(jnp.sum(values, axis=0, keepdims=True), axis=1, keepdims=True)

    stats = jnp.where(lane_s == 8, total(loss_sum), 0.0)
    stats = jnp.where(lane_s == 9, total(temp_sum), stats)
    for k in range(8):
        bucket = total(jnp.where(apart == float(k), by_gap, 0.0))
        stats = jnp.where(lane_s == k, -bucket, stats)

    def share(value, slots, axis):
        here = me[axis]
        slots[here] = value
        return [
            send(slots.at[here], slots.at[here], {axis: k}) for k in range(1, SIZES[axis])
        ]

    def summed(copies, slots):
        for copy in copies:
            copy.wait_recv()
        value = slots[0]
        for k in range(1, slots.shape[0]):
            value = value + slots[k]
        return value

    stat_core = share(stats, st_core, "core")

    x2p.wait_recv()
    x2m.wait_recv()
    dy_send[128:192, :] = (dy[128:192, :] + dy_x2[0:64, :].astype(F32)).astype(BF16)
    dy_send[192:256, :] = dy[192:256, :].astype(BF16)
    x1p = send(dy_send.at[pl.ds(128, 128)], dy_x1.at[pl.ds(0, 128)], {"x": 1})
    dy_send[256:320, :] = dy[384:448, :].astype(BF16)
    dy_send[320:384, :] = (dy[448:512, :] + dy_x2[64:128, :].astype(F32)).astype(BF16)
    x1m = send(dy_send.at[pl.ds(256, 128)], dy_x1.at[pl.ds(128, 128)], {"x": -1})

    stat_z = share(summed(stat_core, st_core), st_z, "z")

    dx_swap.wait_recv()

    def own(k):
        at = pl.ds((k % NZ) * XR, XR)
        return dx[at, :] + dx_core[at, :]

    dx_send[0] = own(3).astype(BF16)
    z3p = send(dx_send.at[0], dx_far.at[0], {"z": 1})
    dx_send[1] = own(-3).astype(BF16)
    z3m = send(dx_send.at[1], dx_far.at[1], {"z": -1})
    dx_send[2] = own(4).astype(BF16)
    z4p = send(dx_send.at[2, pl.ds(0, 16)], dx_half.at[0], {"z": 2})
    z4m = send(dx_send.at[2, pl.ds(16, 16)], dx_half.at[1], {"z": -2})
    dx_send[3] = own(1).astype(BF16)
    z1p = send(dx_send.at[3], dx_near.at[0], {"z": 1})
    dx_send[4] = own(-1).astype(BF16)
    z1m = send(dx_send.at[4], dx_near.at[1], {"z": -1})
    dx_mid[0] = own(2)
    dx_mid[1] = own(-2)
    z3p.wait_recv()
    z4p.wait_recv()
    part = dx_mid[0] + dx_far[0].astype(F32)
    dx_send[5, 0:16] = (part[0:16] + dx_half[0].astype(F32)).astype(BF16)
    dx_send[5, 16:32] = part[16:32].astype(BF16)
    z2p = send(dx_send.at[5], dx_next.at[0], {"z": 2})
    z3m.wait_recv()
    z4m.wait_recv()
    part = dx_mid[1] + dx_far[1].astype(F32)
    dx_send[6, 0:16] = part[0:16].astype(BF16)
    dx_send[6, 16:32] = (part[16:32] + dx_half[1].astype(F32)).astype(BF16)
    z2m = send(dx_send.at[6], dx_next.at[1], {"z": -2})

    stat_y = share(summed(stat_z, st_z), st_y, "y")

    x1p.wait_recv()
    x1m.wait_recv()
    dy_sum[...] = dy[0:128, :] + dy_x1[0:128, :].astype(F32) + dy_x1[128:256, :].astype(F32)

    def part_y(j):
        return dy_sum.at[pl.ds((j % NY) * YR, YR)]

    first, second = pl.ds(0, 512), pl.ds(512, 512)
    y3p = send(part_y(3), dy_far.at[0], {"y": 1})
    y3m = send(part_y(-3), dy_far.at[1], {"y": -1})
    y4p = send(part_y(4).at[:, first], dy_half.at[0], {"y": 2})
    y4m = send(part_y(4).at[:, second], dy_half.at[1], {"y": -2})
    y1p = send(part_y(1), dy_near.at[0], {"y": 1})
    y1m = send(part_y(-1), dy_near.at[1], {"y": -1})

    stat_x = share(summed(stat_y, st_y), st_x, "x")

    y3p.wait_recv()
    y4p.wait_recv()
    near = dy_sum[2 * YR : 3 * YR, :] + dy_far[0]
    dy_mid[0, :, 0:512] = near[:, 0:512] + dy_half[0]
    dy_mid[0, :, 512:1024] = near[:, 512:1024]
    y2p = send(dy_mid.at[0], dy_next.at[0], {"y": 2})
    y3m.wait_recv()
    y4m.wait_recv()
    near = dy_sum[6 * YR : 7 * YR, :] + dy_far[1]
    dy_mid[1, :, 0:512] = near[:, 0:512]
    dy_mid[1, :, 512:1024] = near[:, 512:1024] + dy_half[1]
    y2m = send(dy_mid.at[1], dy_next.at[1], {"y": -2})

    temperature = jnp.exp(jnp.full((XR, D), nef_ref[0], F32))
    for copy in (z1p, z1m, z2p, z2m):
        copy.wait_recv()
    full = own(0) + dx_near[0].astype(F32) + dx_near[1].astype(F32)
    full = full + dx_next[0].astype(F32) + dx_next[1].astype(F32)
    gt_ref[...] = temperature * full

    stats = summed(stat_x, st_x)
    in_bucket = jnp.where(lane_s < 8, stats, 0.0)
    stats = jnp.where(lane_s == 10, -jnp.sum(in_bucket, axis=1, keepdims=True), stats)
    stat_ref[...] = stats * (1.0 / PAIRS)

    for copy in (y1p, y1m, y2p, y2m):
        copy.wait_recv()
    full = dy_sum[0:YR, :] + dy_near[0] + dy_near[1] + dy_next[0] + dy_next[1]
    gw_ref[...] = temperature[0:YR] * full

    for copy in started:
        copy.wait_send()


COPIES = 128


def finish(gt_in, gw_in, stat_in, loss, gt, gw, bias, temp, penalty):
    gt[...] = gt_in[...]
    gw[...] = gw_in[...]
    loss[0] = stat_in[0, 8]
    temp[0] = stat_in[0, 9]
    bias[0] = stat_in[0, 10]
    for k in range(8):
        penalty[k] = stat_in[0, k]


def local(timelines, windows, row_gap, col_gap, positive, nef, bias, deduction):
    vmem = pl.BlockSpec(memory_space=pltpu.VMEM)
    smem = pl.BlockSpec(memory_space=pltpu.SMEM)
    shape = jax.ShapeDtypeStruct
    gt, gw, stats = pl.pallas_call(
        kernel,
        out_shape=(shape((XR, D), F32), shape((YR, D), F32), shape((8, 128), F32)),
        in_specs=[smem] * 3 + [vmem] * 5,
        out_specs=(vmem, vmem, vmem),
        scratch_shapes=[
            pltpu.VMEM((NR, DE), BF16),
            pltpu.VMEM((NW, DE), BF16),
            pltpu.VMEM((NR, 128), BF16),
            pltpu.VMEM((NW, 128), BF16),
            pltpu.VMEM((NR, NW), F32),
            pltpu.VMEM((NR, NW), F32),
            pltpu.VMEM((NR, NW), BF16),
            pltpu.VMEM((NR, NW), BF16),
            pltpu.VMEM((NR, D), F32),
            pltpu.VMEM((HALF, D), F32),
            pltpu.VMEM((7, XR, D), BF16),
            pltpu.VMEM((2, XR, D), BF16),
            pltpu.VMEM((2, 16, D), BF16),
            pltpu.VMEM((2, XR, D), BF16),
            pltpu.VMEM((2, XR, D), F32),
            pltpu.VMEM((2, XR, D), BF16),
            pltpu.VMEM((NW, D), F32),
            pltpu.VMEM((384, D), BF16),
            pltpu.VMEM((128, D), BF16),
            pltpu.VMEM((256, D), BF16),
            pltpu.VMEM((128, D), F32),
            pltpu.VMEM((2, YR, D), F32),
            pltpu.VMEM((2, YR, 512), F32),
            pltpu.VMEM((2, YR, D), F32),
            pltpu.VMEM((2, YR, D), F32),
            pltpu.VMEM((2, YR, D), F32),
            pltpu.VMEM((2, 8, 128), F32),
            pltpu.VMEM((NZ, 8, 128), F32),
            pltpu.VMEM((NY, 8, 128), F32),
            pltpu.VMEM((NX, 8, 128), F32),
            pltpu.SemaphoreType.DMA((COPIES,)),
            pltpu.SemaphoreType.DMA((COPIES,)),
        ],
        compiler_params=pltpu.CompilerParams(
            collective_id=0, has_side_effects=True, vmem_limit_bytes=48 << 20
        ),
        name="loss_and_gradients",
    )(
        nef, bias, deduction,
        timelines, windows.reshape(YR, D), row_gap.reshape(1, XR), positive.reshape(1, XR), col_gap,
    )
    loss, gt, gw, g_bias, g_temp, g_pen = pl.pallas_call(
        finish,
        out_shape=(
            shape((1,), F32), shape((XR, D), F32), shape((YR, D), F32),
            shape((1,), F32), shape((1,), F32), shape((8,), F32),
        ),
        in_specs=[vmem, vmem, smem],
        out_specs=(smem, vmem, vmem, smem, smem, smem),
        name="finish",
    )(gt, gw, stats)
    return loss, gt, gw.reshape(YR, 1, D), g_bias, g_temp, g_pen


def solution(mesh):
    return jax.shard_map(
        local,
        mesh=mesh,
        in_specs=(
            P(("row", "col"), None),
            P("row", "col", None),
            P(("row", "col")),
            P("row", "col"),
            P(("row", "col")),
            P(),
            P(),
            P(),
        ),
        out_specs=(P(), P(("row", "col"), None), P("row", "col", None), P(), P(), P()),
        check_vma=False,
    )
```

```python
import jax
import jax.numpy as jnp
from jax import lax
from jax.experimental import pallas as pl
from jax.experimental.pallas import tpu as pltpu
from jax.sharding import PartitionSpec as P

MESH = pl.DeviceIdType.MESH
F32 = jnp.float32
BF16 = jnp.bfloat16

D = 1024
DE = D + 128
XR = 32
YR = 16
NZ, NY, NX = 8, 8, 4
NR = XR * NZ * 2
NW = YR * NY * NX
HALF = NR // 2
PAIRS = 134217728
SIZES = {"core": 2, "x": NX, "y": NY, "z": NZ}
GROUP = [(axis, k) for axis in SIZES for k in range(1, SIZES[axis])]
PLACE = (0, 1, 3, 2)
NT = (((1,), (1,)), ((), ()))
TN = (((0,), (0,)), ((), ()))


def position():
    row, col = lax.axis_index("row"), lax.axis_index("col")
    return {
        "core": lax.rem(row, 2),
        "y": lax.rem(lax.div(row, 2), NY),
        "x": lax.div(row, 2 * NY) * 2 + lax.rem(col, 2),
        "z": lax.div(col, 2),
    }


def device(me, axis, k):
    at = dict(me)
    at[axis] = lax.rem(me[axis] + (k + SIZES[axis]), SIZES[axis])
    row = lax.div(at["x"], 2) * (2 * NY) + at["y"] * 2 + at["core"]
    return (row, at["z"] * 2 + lax.rem(at["x"], 2))


def dot(a, b, dims):
    return lax.dot_general(a, b, dims, preferred_element_type=F32)


def kernel(
    nef_ref, bias_ref, ded_in, t_ref, w_ref, gap_in, pos_in, colgap_in,
    out_ref,
    ded_ref, gap_ref, pos_ref, colgap_ref,
    xg, yg, oh, pt, sim, dm, slope, slope_lo,
    dx, dx_core, dx_send, dx_far, dx_half, dx_near, dx_mid, dx_next,
    dy, x2_send, x2_recv, x1_send, x1_recv, y_send, y_recv,
    st_core, st_z, st_y, st_x,
    local_sem, send_sem, recv_sem,
):
    me = position()
    ids = {(axis, k): device(me, axis, k) for axis, k in GROUP}
    barrier = pltpu.get_barrier_semaphore()
    for there in ids.values():
        pl.semaphore_signal(barrier, inc=1, device_id=there, device_id_type=MESH)

    fetched = []
    for src, dst in (
        (gap_in, gap_ref),
        (pos_in, pos_ref),
        (colgap_in, colgap_ref),
        (w_ref, yg.at[pl.ds(0, YR), pl.ds(0, D)]),
        (t_ref, xg.at[pl.ds(0, XR), pl.ds(0, D)]),
        (ded_in, ded_ref),
    ):
        copy = pltpu.make_async_copy(src, dst, local_sem.at[len(fetched)])
        copy.start()
        fetched.append(copy)

    started = []

    def send(src, dst, axis, k):
        i = len(started)
        copy = pltpu.make_async_remote_copy(
            src_ref=src,
            dst_ref=dst,
            send_sem=send_sem.at[i],
            recv_sem=recv_sem.at[i],
            device_id=ids[axis, k % SIZES[axis]],
            device_id_type=MESH,
        )
        copy.start()
        started.append(copy)
        return copy

    for copy in fetched:
        copy.wait()
    lane = lax.broadcasted_iota(jnp.int32, (XR, 128), 1)

    def column(ref, n):
        diagonal = lax.broadcasted_iota(jnp.int32, (n, n), 0) == lax.broadcasted_iota(
            jnp.int32, (n, n), 1
        )
        row = jnp.broadcast_to(ref[...].astype(F32), (n, n))
        return jnp.sum(jnp.where(diagonal, row, 0.0), axis=1, keepdims=True)

    gap, pos = column(gap_ref, XR), column(pos_ref, XR)
    pos_high = jnp.floor(pos * (1.0 / 128.0))
    pos_low = pos - 128.0 * pos_high
    extra = jnp.where(
        lane == 0, gap, jnp.where(lane == 1, pos_high, jnp.where(lane == 2, pos_low, 0.0))
    )
    xg[0:XR, D:DE] = extra.astype(BF16)
    yg[0:YR, D:DE] = jnp.broadcast_to(column(colgap_ref, YR), (YR, 128)).astype(BF16)

    pl.semaphore_wait(barrier, len(GROUP))

    def xs(k):
        return xg.at[pl.ds((k % NZ) * XR, XR)]

    def xs_other(k):
        return xg.at[pl.ds(HALF + (k % NZ) * XR, XR)]

    def ys(i, j):
        return yg.at[pl.ds((PLACE[i % NX] * NY + j % NY) * YR, YR)]

    lo_cols, hi_cols = pl.ds(0, 512), pl.ds(512, DE - 512)
    xp, xm, core, far = {}, {}, {}, []

    def to_x(j):
        xp[j] = send(ys(0, j), ys(-1, j), "x", 1)
        xm[j] = send(ys(0, j), ys(1, j), "x", -1)

    def to_core(k):
        core[k] = send(xs(k), xs_other(k), "core", 1)

    by_plus, order = (0, -2, -1, -3), (0, -1, 1, -2, 2, -3, 3, 4)

    def onward(j):
        if j in by_plus:
            xp[j].wait_recv()
            far.append(send(ys(-1, j), ys(2, j), "x", 1))
        else:
            xm[j].wait_recv()
            far.append(send(ys(1, j), ys(2, j), "x", -1))

    yp1 = send(ys(0, 0), ys(0, -1), "y", 1)
    ym1 = send(ys(0, 0), ys(0, 1), "y", -1)
    yp2 = send(ys(0, 0), ys(0, -2), "y", 2)
    ym2 = send(ys(0, 0), ys(0, 2), "y", -2)
    to_x(0)
    zp2 = send(xs(0), xs(-2), "z", 2)
    zm2 = send(xs(0), xs(2), "z", -2)
    zp1 = send(xs(0), xs(-1), "z", 1)
    zm1 = send(xs(0), xs(1), "z", -1)
    to_core(0)

    yp1.wait_recv()
    to_x(-1)
    ym1.wait_recv()
    to_x(1)
    onward(0)
    yp2.wait_recv()
    yp4 = send(ys(0, -2).at[:, lo_cols], ys(0, 4).at[:, lo_cols], "y", 2)
    yp3 = send(ys(0, -2), ys(0, -3), "y", 1)
    to_x(-2)
    ym2.wait_recv()
    ym4 = send(ys(0, 2).at[:, hi_cols], ys(0, 4).at[:, hi_cols], "y", -2)
    ym3 = send(ys(0, 2), ys(0, 3), "y", -1)
    to_x(2)
    zp2.wait_recv()
    zp4 = send(xs(-2).at[pl.ds(0, 16)], xs(4).at[pl.ds(0, 16)], "z", 2)
    zp3 = send(xs(-2), xs(-3), "z", 1)
    zm2.wait_recv()
    zm4 = send(xs(2).at[pl.ds(16, 16)], xs(4).at[pl.ds(16, 16)], "z", -2)
    zm3 = send(xs(2), xs(3), "z", -1)
    onward(-1)
    onward(1)
    to_core(-2)
    to_core(2)
    zp1.wait_recv()
    to_core(-1)
    zm1.wait_recv()
    to_core(1)
    yp3.wait_recv()
    to_x(-3)
    ym3.wait_recv()
    to_x(3)
    yp4.wait_recv()
    ym4.wait_recv()
    to_x(4)
    onward(-2)
    onward(2)
    zp3.wait_recv()
    to_core(-3)
    zm3.wait_recv()
    to_core(3)
    zp4.wait_recv()
    zm4.wait_recv()
    to_core(4)
    onward(-3)
    onward(3)
    onward(4)

    lane = lax.broadcasted_iota(jnp.int32, (64, 128), 1)
    lane16 = (lane % 16).astype(F32)
    bias = jnp.broadcast_to(bias_ref[...], (64, 128))

    for copy in core.values():
        copy.wait_recv()

    def one_hot(b, _):
        at = pl.ds(pl.multiple_of(b * 64, 64), 64)
        mine = xg[at, D:DE].astype(F32)[:, 0:1]
        oh[at, :] = jnp.where((lane16 == mine) & (lane < 48), 1.0, 0.0).astype(BF16)
        return 0

    lax.fori_loop(0, NR // 64, one_hot, 0)

    def tables(b, _):
        at = pl.ds(pl.multiple_of(b * 64, 64), 64)
        apart = jnp.abs(lane16 - yg[at, D:DE].astype(F32))
        table = jnp.full((64, 128), ded_ref[7], F32)
        for k in range(7):
            table = jnp.where(apart == float(k), ded_ref[k], table)
        table = table - bias
        first = table.astype(BF16)
        rest = table - first.astype(F32)
        second = rest.astype(BF16)
        third = (rest - second.astype(F32)).astype(BF16)
        pt[at, :] = jnp.where(
            lane < 16,
            first.astype(F32),
            jnp.where(lane < 32, second.astype(F32), jnp.where(lane < 48, third.astype(F32), 0.0)),
        ).astype(BF16)
        return 0

    def group(lo, hi, step, sums):
        n = hi - lo
        lax.fori_loop(lo // 64, hi // 64, tables, 0)

        def products(b, _):
            at = pl.ds(pl.multiple_of(b * 256, 256), 256)
            sim[at, lo:hi] = dot(xg[at, 0:D], yg[lo:hi, 0:D], NT)
            dm[at, lo:hi] = dot(oh[at, :], pt[lo:hi, :], NT)
            return 0

        lax.fori_loop(0, NR // 256, products, 0)
        scale = jnp.exp(jnp.broadcast_to(nef_ref[...], (step, n)))
        at_lane = lax.broadcasted_iota(jnp.int32, (1, n), 1) + lo
        place = at_lane // (YR * NY)
        from_x = jnp.where(place == 2, 3, jnp.where(place == 3, 2, place))
        win_y = (at_lane // YR + me["y"]) % NY
        win_x = (from_x + me["x"]) % NX
        win_row = (win_x // 2) * (2 * NY) + win_y * 2 + me["core"]
        ordinal = (me["z"] * 2 + win_x % 2) * 512 + win_row * YR + at_lane % YR
        ordinal = ordinal.astype(F32)

        def slopes(b, sums):
            at = pl.ds(pl.multiple_of(b * step, step), step)
            loss_sum, temp_sum = sums
            s = scale * sim[at, lo:hi]
            logit = s - dm[at, lo:hi]
            mine = xg[at, D:DE].astype(F32)
            match = (mine[:, 1:2] * 128.0 + mine[:, 2:3]) == ordinal
            z = jnp.where(match, -logit, logit)
            e = jnp.exp(-jnp.abs(z))
            r = 1.0 / (1.0 + e)
            sig = jnp.where(z >= 0.0, r, e * r)
            grad = jnp.where(match, -sig, sig)
            loss = jnp.maximum(z, 0.0) + jnp.log1p(e)
            temp = grad * s
            high = grad.astype(BF16)
            slope[at, lo:hi] = high
            slope_lo[at, lo:hi] = (grad - high.astype(F32)).astype(BF16)
            for i in range(0, step, 16):
                for j in range(0, n, 128):
                    loss_sum = loss_sum + loss[i : i + 16, j : j + 128]
                    temp_sum = temp_sum + temp[i : i + 16, j : j + 128]
            return loss_sum, temp_sum

        return lax.fori_loop(0, NR // step, slopes, sums)

    for j in order:
        if j not in (-3, 3, 4):
            (xm if j in by_plus else xp)[j].wait_recv()
    for j in (-3, 3, 4):
        (xm if j in by_plus else xp)[j].wait_recv()
    zero = jnp.zeros((16, 128), F32)
    sums = group(0, 384, 16, (zero, zero))
    for copy in far:
        copy.wait_recv()
    loss_sum, temp_sum = group(384, 512, 32, sums)

    def win_grad(lo, hi):
        def columns(b, _):
            at = pl.ds(pl.multiple_of(b * 256, 256), 256)
            dy[lo:hi, at] = dot(slope[:, lo:hi], xg[:, at], TN)
            return 0

        lax.fori_loop(0, D // 256, columns, 0)

    def time_grad(lo):
        def columns(b, _):
            at = pl.ds(pl.multiple_of(b * 256, 256), 256)
            dx[lo : lo + HALF, at] = dot(slope[lo : lo + HALF, :], yg[:, at], (((1,), (0,)), ((), ())))
            return 0

        lax.fori_loop(0, D // 256, columns, 0)

    def pair(j):
        return pl.ds(j * YR, 2 * YR)

    win_grad(384, 512)
    x2_send[...] = dy[384:512, :].astype(BF16)
    x2 = {}
    for j in (2, 4, 0, 6):
        x2[j] = send(x2_send.at[pair(j)], x2_recv.at[pair(j)], "x", 1 if j < 4 else -1)

    by_gap = dot(slope[...], oh[...], TN) + dot(slope_lo[...], oh[...], TN)
    lane_w = lax.broadcasted_iota(jnp.int32, (NW, 128), 1)
    apart = jnp.abs((lane_w % 16).astype(F32) - yg[:, D:DE].astype(F32))
    apart = jnp.where(lane_w < 16, jnp.minimum(apart, 7.0), 8.0)
    lane_s = lax.broadcasted_iota(jnp.int32, (8, 128), 1)

    def total(values):
        return jnp.sum(jnp.sum(values, axis=0, keepdims=True), axis=1, keepdims=True)

    stats = jnp.where(lane_s == 8, total(loss_sum), 0.0)
    stats = jnp.where(lane_s == 9, total(temp_sum), stats)
    for k in range(8):
        bucket = total(jnp.where(apart == float(k), by_gap, 0.0))
        stats = jnp.where(lane_s == k, -bucket, stats)

    def share(value, slots, axis):
        here = me[axis]
        slots[here] = value
        return [send(slots.at[here], slots.at[here], axis, k) for k in range(1, SIZES[axis])]

    def summed(copies, slots):
        for copy in copies:
            copy.wait_recv()
        value = slots[0]
        for k in range(1, slots.shape[0]):
            value = value + slots[k]
        return value

    stat_core = share(stats, st_core, "core")

    time_grad(HALF)
    dx_swap = send(dx.at[pl.ds(HALF, HALF)], dx_core, "core", 1)

    win_grad(128, 384)
    x1 = {}

    def x1_to(side, j, passing):
        part = dy[128 + side * 128 + j * YR : 128 + side * 128 + (j + 2) * YR, :]
        if passing:
            x2[j].wait_recv()
            part = part + x2_recv[j * YR : (j + 2) * YR, :].astype(F32)
        x1_send[side, j * YR : (j + 2) * YR, :] = part.astype(BF16)
        x1[side, j] = send(
            x1_send.at[side, pair(j)], x1_recv.at[side, pair(j)], "x", 1 if side == 0 else -1
        )

    x1_to(0, 4, False)
    x1_to(1, 2, False)
    stat_y = share(summed(stat_core, st_core), st_y, "y")
    time_grad(0)
    x1_to(0, 2, True)
    x1_to(1, 4, True)
    x1_to(0, 6, False)
    x1_to(1, 0, False)
    win_grad(0, 128)
    x1_to(0, 0, True)
    x1_to(1, 6, True)

    dx_swap.wait_recv()

    def own(k):
        at = pl.ds((k % NZ) * XR, XR)
        return dx[at, :] + dx_core[at, :]

    dx_send[0] = own(3).astype(BF16)
    z3p = send(dx_send.at[0], dx_far.at[0], "z", 1)
    dx_send[1] = own(-3).astype(BF16)
    z3m = send(dx_send.at[1], dx_far.at[1], "z", -1)
    dx_send[2] = own(4).astype(BF16)
    z4p = send(dx_send.at[2, pl.ds(0, 16)], dx_half.at[0], "z", 2)
    z4m = send(dx_send.at[2, pl.ds(16, 16)], dx_half.at[1], "z", -2)
    stat_z = share(summed(stat_y, st_y), st_z, "z")
    dx_send[3] = own(1).astype(BF16)
    z1p = send(dx_send.at[3], dx_near.at[0], "z", 1)
    dx_send[4] = own(-1).astype(BF16)
    z1m = send(dx_send.at[4], dx_near.at[1], "z", -1)
    dx_mid[0] = own(2)
    dx_mid[1] = own(-2)

    ysent = []

    def along_y(j):
        at = slice(j * YR, (j + 1) * YR)
        part = dy[at, :] + x1_recv[0, at, :].astype(F32) + x1_recv[1, at, :].astype(F32)
        y_send[j] = part.astype(BF16)
        ysent.append(send(y_send.at[j], y_recv.at[j], "y", j))

    z3p.wait_recv()
    z4p.wait_recv()
    part = dx_mid[0] + dx_far[0].astype(F32)
    dx_send[5, 0:16] = (part[0:16] + dx_half[0].astype(F32)).astype(BF16)
    dx_send[5, 16:32] = part[16:32].astype(BF16)
    z2p = send(dx_send.at[5], dx_next.at[0], "z", 2)
    z3m.wait_recv()
    z4m.wait_recv()
    part = dx_mid[1] + dx_far[1].astype(F32)
    dx_send[6, 0:16] = part[0:16].astype(BF16)
    dx_send[6, 16:32] = (part[16:32] + dx_half[1].astype(F32)).astype(BF16)
    z2m = send(dx_send.at[6], dx_next.at[1], "z", -2)

    x1[1, 4].wait_recv()
    x1[0, 4].wait_recv()
    along_y(4)
    along_y(5)
    x1[0, 2].wait_recv()
    x1[1, 2].wait_recv()
    along_y(3)
    along_y(2)
    stat_x = share(summed(stat_z, st_z), st_x, "x")
    x1[0, 6].wait_recv()
    x1[1, 6].wait_recv()
    along_y(6)
    along_y(7)
    x1[0, 0].wait_recv()
    x1[1, 0].wait_recv()
    along_y(1)
    mine = dy[0:YR, :] + x1_recv[0, 0:YR, :].astype(F32) + x1_recv[1, 0:YR, :].astype(F32)

    temperature = jnp.exp(jnp.broadcast_to(nef_ref[...], (XR, D)))
    for copy in (z1p, z1m, z2p, z2m):
        copy.wait_recv()
    full = own(0) + dx_near[0].astype(F32) + dx_near[1].astype(F32)
    full = full + dx_next[0].astype(F32) + dx_next[1].astype(F32)
    out_ref[0:XR, :] = temperature * full

    stats = summed(stat_x, st_x) * (1.0 / PAIRS)
    in_bucket = jnp.where(lane_s < 8, stats, 0.0)
    row_s = lax.broadcasted_iota(jnp.int32, (8, 128), 0)
    stats = jnp.where(
        row_s == 1,
        stats[:, 8:9],
        jnp.where(
            row_s == 2,
            stats[:, 9:10],
            jnp.where(row_s == 3, -jnp.sum(in_bucket, axis=1, keepdims=True), stats),
        ),
    )
    out_ref[XR + YR : XR + YR + 8, 0:128] = stats

    for copy in ysent:
        copy.wait_recv()
    for j in range(1, NY):
        mine = mine + y_recv[j].astype(F32)
    out_ref[XR : XR + YR, :] = temperature[0:YR] * mine

    for copy in started:
        copy.wait_send()


COPIES = 140


def finish(packed, loss, gt, gw, bias, temp, penalty):
    gt[...] = packed[0:XR, :]
    gw[...] = packed[XR : XR + YR, :].reshape(YR, 1, D)
    penalty[...] = packed[XR + YR, 0:8]
    loss[...] = packed[XR + YR + 1, 0:1]
    temp[...] = packed[XR + YR + 2, 0:1]
    bias[...] = packed[XR + YR + 3, 0:1]


def local(timelines, windows, row_gap, col_gap, positive, nef, bias, deduction):
    vmem = pl.BlockSpec(memory_space=pltpu.VMEM)
    anywhere = pl.BlockSpec(memory_space=pltpu.HBM)
    shape = jax.ShapeDtypeStruct
    packed = pl.pallas_call(
        kernel,
        out_shape=shape((XR + YR + 8, D), F32),
        in_specs=[vmem] * 2 + [anywhere] * 6,
        out_specs=vmem,
        scratch_shapes=[
            pltpu.SMEM((8,), F32),
            pltpu.VMEM((1, XR), jnp.int32),
            pltpu.VMEM((1, XR), jnp.int32),
            pltpu.VMEM((1, YR), jnp.int32),
            pltpu.VMEM((NR, DE), BF16),
            pltpu.VMEM((NW, DE), BF16),
            pltpu.VMEM((NR, 128), BF16),
            pltpu.VMEM((NW, 128), BF16),
            pltpu.VMEM((NR, NW), F32),
            pltpu.VMEM((NR, NW), F32),
            pltpu.VMEM((NR, NW), BF16),
            pltpu.VMEM((NR, NW), BF16),
            pltpu.VMEM((NR, D), F32),
            pltpu.VMEM((HALF, D), F32),
            pltpu.VMEM((7, XR, D), BF16),
            pltpu.VMEM((2, XR, D), BF16),
            pltpu.VMEM((2, 16, D), BF16),
            pltpu.VMEM((2, XR, D), BF16),
            pltpu.VMEM((2, XR, D), F32),
            pltpu.VMEM((2, XR, D), BF16),
            pltpu.VMEM((NW, D), F32),
            pltpu.VMEM((128, D), BF16),
            pltpu.VMEM((128, D), BF16),
            pltpu.VMEM((2, 128, D), BF16),
            pltpu.VMEM((2, 128, D), BF16),
            pltpu.VMEM((NY, YR, D), BF16),
            pltpu.VMEM((NY, YR, D), BF16),
            pltpu.VMEM((2, 8, 128), F32),
            pltpu.VMEM((NZ, 8, 128), F32),
            pltpu.VMEM((NY, 8, 128), F32),
            pltpu.VMEM((NX, 8, 128), F32),
            pltpu.SemaphoreType.DMA((6,)),
            pltpu.SemaphoreType.DMA((COPIES,)),
            pltpu.SemaphoreType.DMA((COPIES,)),
        ],
        compiler_params=pltpu.CompilerParams(
            collective_id=0, has_side_effects=True, vmem_limit_bytes=56 << 20
        ),
        name="loss_and_gradients",
    )(
        nef.reshape(1, 1), bias.reshape(1, 1), deduction, timelines, windows.reshape(YR, D),
        row_gap.reshape(1, XR), positive.reshape(1, XR), col_gap.reshape(1, YR),
    )
    return pl.pallas_call(
        finish,
        out_shape=(
            shape((1,), F32), shape((XR, D), F32), shape((YR, 1, D), F32),
            shape((1,), F32), shape((1,), F32), shape((8,), F32),
        ),
        in_specs=[vmem],
        out_specs=(vmem,) * 6,
        name="finish",
    )(packed)


def solution(mesh):
    return jax.shard_map(
        local,
        mesh=mesh,
        in_specs=(
            P(("row", "col"), None),
            P("row", "col", None),
            P(("row", "col")),
            P("row", "col"),
            P(("row", "col")),
            P(),
            P(),
            P(),
        ),
        out_specs=(P(), P(("row", "col"), None), P("row", "col", None), P(), P(), P()),
        check_vma=False,
    )
```

```python
import jax
import jax.numpy as jnp
from jax import lax
from jax.experimental import pallas as pl
from jax.experimental.pallas import tpu as pltpu
from jax.sharding import PartitionSpec as P

MESH = pl.DeviceIdType.MESH
F32 = jnp.float32
BF16 = jnp.bfloat16

D = 1024
DE = D + 128
XR = 32
YR = 16
NZ, NY, NX = 8, 8, 4
NR = XR * NZ * 2
NW = YR * NY * NX
HALF = NR // 2
PAIRS = 134217728
SIZES = {"core": 2, "x": NX, "y": NY, "z": NZ}
GROUP = [(axis, k) for axis in SIZES for k in range(1, SIZES[axis])]
NEAR = [(axis, k) for axis, k in GROUP if min(k, SIZES[axis] - k) <= (1 if axis == "x" else 2)]
PLACE = (0, 1, 3, 2)
NT = (((1,), (1,)), ((), ()))
TN = (((0,), (0,)), ((), ()))
NN = (((1,), (0,)), ((), ()))


def position():
    row, col = lax.axis_index("row"), lax.axis_index("col")
    return {
        "core": lax.rem(row, 2),
        "y": lax.rem(lax.div(row, 2), NY),
        "x": lax.div(row, 2 * NY) * 2 + lax.rem(col, 2),
        "z": lax.div(col, 2),
    }


def device(me, axis, k):
    at = dict(me)
    at[axis] = lax.rem(me[axis] + (k + SIZES[axis]), SIZES[axis])
    row = lax.div(at["x"], 2) * (2 * NY) + at["y"] * 2 + at["core"]
    return (row, at["z"] * 2 + lax.rem(at["x"], 2))


def dot(a, b, dims):
    return lax.dot_general(a, b, dims, preferred_element_type=F32)


def kernel(
    nef_ref, bias_ref, ded_in, t_ref, w_ref, gap_in, pos_in, colgap_in,
    out_ref,
    ded_ref, gap_ref, pos_ref, colgap_ref,
    xg, yg, oh, pt, sim, dm, slope, slope_lo,
    dx, dx_core, dx_send, dx_far, dx_half, dx_near, dx_mid, dx_next,
    dy, x2_send, x2_recv, x1_send, x1_recv, y_send, y_recv,
    st_core, st_z, st_y, st_x,
    local_sem, send_sem, recv_sem,
):
    me = position()
    ids = {(axis, k): device(me, axis, k) for axis, k in GROUP}
    barrier = pltpu.get_barrier_semaphore()
    for near in NEAR:
        pl.semaphore_signal(barrier, inc=1, device_id=ids[near], device_id_type=MESH)

    fetched = []
    for src, dst in (
        (gap_in, gap_ref),
        (pos_in, pos_ref),
        (colgap_in, colgap_ref),
        (w_ref, yg.at[pl.ds(0, YR), pl.ds(0, D)]),
        (t_ref, xg.at[pl.ds(0, XR), pl.ds(0, D)]),
        (ded_in, ded_ref),
    ):
        copy = pltpu.make_async_copy(src, dst, local_sem.at[len(fetched)])
        copy.start()
        fetched.append(copy)

    started = []

    def send(src, dst, axis, k):
        i = len(started)
        copy = pltpu.make_async_remote_copy(
            src_ref=src,
            dst_ref=dst,
            send_sem=send_sem.at[i],
            recv_sem=recv_sem.at[i],
            device_id=ids[axis, k % SIZES[axis]],
            device_id_type=MESH,
        )
        copy.start()
        started.append(copy)
        return copy

    for copy in fetched:
        copy.wait()
    lane = lax.broadcasted_iota(jnp.int32, (XR, 128), 1)

    def column(ref, n):
        diagonal = lax.broadcasted_iota(jnp.int32, (n, n), 0) == lax.broadcasted_iota(
            jnp.int32, (n, n), 1
        )
        row = jnp.broadcast_to(ref[...].astype(F32), (n, n))
        return jnp.sum(jnp.where(diagonal, row, 0.0), axis=1, keepdims=True)

    gap, pos = column(gap_ref, XR), column(pos_ref, XR)
    pos_high = jnp.floor(pos * (1.0 / 128.0))
    pos_low = pos - 128.0 * pos_high
    extra = jnp.where(
        lane == 0, gap, jnp.where(lane == 1, pos_high, jnp.where(lane == 2, pos_low, 0.0))
    )
    xg[0:XR, D:DE] = extra.astype(BF16)
    yg[0:YR, D:DE] = jnp.broadcast_to(column(colgap_ref, YR), (YR, 128)).astype(BF16)

    pl.semaphore_wait(barrier, len(NEAR))

    def xs(k):
        return xg.at[pl.ds((k % NZ) * XR, XR)]

    def xs_other(k):
        return xg.at[pl.ds(HALF + (k % NZ) * XR, XR)]

    def ys(i, j):
        return yg.at[pl.ds((PLACE[i % NX] * NY + j % NY) * YR, YR)]

    lo_cols, hi_cols = pl.ds(0, 512), pl.ds(512, DE - 512)
    xp, xm, core, far = {}, {}, {}, []

    def to_x(j):
        xp[j] = send(ys(0, j), ys(-1, j), "x", 1)
        xm[j] = send(ys(0, j), ys(1, j), "x", -1)

    def to_core(k):
        core[k] = send(xs(k), xs_other(k), "core", 1)

    by_plus, order = (0, -2, -1, -3), (0, -1, 1, -2, 2, -3, 3, 4)

    def onward(j):
        if j in by_plus:
            xp[j].wait_recv()
            far.append(send(ys(-1, j), ys(2, j), "x", 1))
        else:
            xm[j].wait_recv()
            far.append(send(ys(1, j), ys(2, j), "x", -1))

    yp1 = send(ys(0, 0), ys(0, -1), "y", 1)
    ym1 = send(ys(0, 0), ys(0, 1), "y", -1)
    yp2 = send(ys(0, 0), ys(0, -2), "y", 2)
    ym2 = send(ys(0, 0), ys(0, 2), "y", -2)
    to_x(0)
    zp2 = send(xs(0), xs(-2), "z", 2)
    zm2 = send(xs(0), xs(2), "z", -2)
    zp1 = send(xs(0), xs(-1), "z", 1)
    zm1 = send(xs(0), xs(1), "z", -1)
    to_core(0)

    yp1.wait_recv()
    to_x(-1)
    ym1.wait_recv()
    to_x(1)
    onward(0)
    yp2.wait_recv()
    yp4 = send(ys(0, -2).at[:, lo_cols], ys(0, 4).at[:, lo_cols], "y", 2)
    yp3 = send(ys(0, -2), ys(0, -3), "y", 1)
    to_x(-2)
    ym2.wait_recv()
    ym4 = send(ys(0, 2).at[:, hi_cols], ys(0, 4).at[:, hi_cols], "y", -2)
    ym3 = send(ys(0, 2), ys(0, 3), "y", -1)
    to_x(2)
    zp2.wait_recv()
    zp4 = send(xs(-2).at[pl.ds(0, 16)], xs(4).at[pl.ds(0, 16)], "z", 2)
    zp3 = send(xs(-2), xs(-3), "z", 1)
    zm2.wait_recv()
    zm4 = send(xs(2).at[pl.ds(16, 16)], xs(4).at[pl.ds(16, 16)], "z", -2)
    zm3 = send(xs(2), xs(3), "z", -1)
    onward(-1)
    onward(1)
    to_core(-2)
    to_core(2)
    zp1.wait_recv()
    to_core(-1)
    zm1.wait_recv()
    to_core(1)
    yp3.wait_recv()
    to_x(-3)
    ym3.wait_recv()
    to_x(3)
    yp4.wait_recv()
    ym4.wait_recv()
    to_x(4)
    onward(-2)
    onward(2)
    zp3.wait_recv()
    to_core(-3)
    zm3.wait_recv()
    to_core(3)
    zp4.wait_recv()
    zm4.wait_recv()
    to_core(4)
    onward(-3)
    onward(3)
    onward(4)

    for copy in core.values():
        copy.wait_recv()
    lane = lax.broadcasted_iota(jnp.int32, (NR, 128), 1)
    lane16 = (lane % 16).astype(F32)
    gap = xg[:, D:DE].astype(F32)[:, 0:1]
    oh[...] = jnp.where((lane16 == gap) & (lane < 48), 1.0, 0.0).astype(BF16)

    def tables(lo, hi):
        lane = lax.broadcasted_iota(jnp.int32, (hi - lo, 128), 1)
        apart = jnp.abs((lane % 16).astype(F32) - yg[lo:hi, D:DE].astype(F32))
        table = jnp.full((hi - lo, 128), ded_ref[7], F32)
        for k in range(7):
            table = jnp.where(apart == float(k), ded_ref[k], table)
        table = table - jnp.broadcast_to(bias_ref[...], (hi - lo, 128))
        first = table.astype(BF16)
        rest = table - first.astype(F32)
        second = rest.astype(BF16).astype(F32)
        third = (rest - second).astype(BF16).astype(F32)
        terms = jnp.where(lane < 32, second, jnp.where(lane < 48, third, 0.0))
        pt[lo:hi, :] = jnp.where(lane < 16, first.astype(F32), terms).astype(BF16)

    def group(lo, hi, step, sums):
        n = hi - lo
        tables(lo, hi)
        sim[:, lo:hi] = dot(xg[:, 0:D], yg[lo:hi, 0:D], NT)
        dm[:, lo:hi] = dot(oh[...], pt[lo:hi, :], NT)
        scale = jnp.exp(jnp.broadcast_to(nef_ref[...], (step, n)))
        at_lane = lax.broadcasted_iota(jnp.int32, (1, n), 1) + lo
        place = at_lane // (YR * NY)
        from_x = jnp.where(place == 2, 3, jnp.where(place == 3, 2, place))
        win_y = (at_lane // YR + me["y"]) % NY
        win_x = (from_x + me["x"]) % NX
        win_row = (win_x // 2) * (2 * NY) + win_y * 2 + me["core"]
        ordinal = (me["z"] * 2 + win_x % 2) * 512 + win_row * YR + at_lane % YR
        ordinal = ordinal.astype(F32)

        def slopes(b, sums):
            at = pl.ds(pl.multiple_of(b * step, step), step)
            loss_sum, temp_sum = sums
            s = scale * sim[at, lo:hi]
            logit = s - dm[at, lo:hi]
            mine = xg[at, D:DE].astype(F32)
            match = (mine[:, 1:2] * 128.0 + mine[:, 2:3]) == ordinal
            z = jnp.where(match, -logit, logit)
            e = jnp.exp(-jnp.abs(z))
            r = 1.0 / (1.0 + e)
            sig = jnp.where(z >= 0.0, r, e * r)
            grad = jnp.where(match, -sig, sig)
            loss = jnp.maximum(z, 0.0) + jnp.log1p(e)
            temp = grad * s
            high = grad.astype(BF16)
            slope[at, lo:hi] = high
            slope_lo[at, lo:hi] = (grad - high.astype(F32)).astype(BF16)
            for i in range(0, step, 16):
                for j in range(0, n, 128):
                    loss_sum = loss_sum + loss[i : i + 16, j : j + 128]
                    temp_sum = temp_sum + temp[i : i + 16, j : j + 128]
            return loss_sum, temp_sum

        return lax.fori_loop(0, NR // step, slopes, sums)

    for j in order:
        if j not in (-3, 3, 4):
            (xm if j in by_plus else xp)[j].wait_recv()
    for j in (-3, 3, 4):
        (xm if j in by_plus else xp)[j].wait_recv()
    zero = jnp.zeros((16, 128), F32)
    sums = group(0, 384, 128, (zero, zero))
    for copy in far:
        copy.wait_recv()
    loss_sum, temp_sum = group(384, 512, 256, sums)

    def win_grad(lo, hi):
        dy[lo:hi, :] = dot(slope[:, lo:hi], xg[:, 0:D], TN)

    def time_grad(lo):
        dx[lo : lo + HALF, :] = dot(slope[lo : lo + HALF, :], yg[:, 0:D], NN)

    def pair(j):
        return pl.ds(j * YR, 2 * YR)

    win_grad(384, 512)
    x2_send[...] = dy[384:512, :].astype(BF16)
    x2 = {}
    for j in (2, 4, 0, 6):
        x2[j] = send(x2_send.at[pair(j)], x2_recv.at[pair(j)], "x", 1 if j < 4 else -1)

    def share(value, slots, axis):
        here = me[axis]
        slots[here] = value
        return [send(slots.at[here], slots.at[here], axis, k) for k in range(1, SIZES[axis])]

    def summed(copies, slots):
        for copy in copies:
            copy.wait_recv()
        value = slots[0]
        for k in range(1, slots.shape[0]):
            value = value + slots[k]
        return value

    time_grad(HALF)
    swaps = []
    for lo, n in ((3, 3), (1, 2), (6, 2), (0, 1)):
        at, to = pl.ds(HALF + lo * XR, n * XR), pl.ds(lo * XR, n * XR)
        swaps.append(send(dx.at[at], dx_core.at[to], "core", 1))

    win_grad(128, 384)
    x1 = {}

    def x1_to(side, j, passing):
        part = dy[128 + side * 128 + j * YR : 128 + side * 128 + (j + 2) * YR, :]
        if passing:
            x2[j].wait_recv()
            part = part + x2_recv[j * YR : (j + 2) * YR, :].astype(F32)
        x1_send[side, j * YR : (j + 2) * YR, :] = part.astype(BF16)
        x1[side, j] = send(
            x1_send.at[side, pair(j)], x1_recv.at[side, pair(j)], "x", 1 if side == 0 else -1
        )

    x1_to(0, 4, False)
    x1_to(1, 2, False)
    time_grad(0)

    def own(k):
        at = pl.ds((k % NZ) * XR, XR)
        return dx[at, :] + dx_core[at, :]

    swaps[0].wait_recv()
    dx_send[0] = own(3).astype(BF16)
    z3p = send(dx_send.at[0], dx_far.at[0], "z", 1)
    dx_send[1] = own(-3).astype(BF16)
    z3m = send(dx_send.at[1], dx_far.at[1], "z", -1)
    dx_send[2] = own(4).astype(BF16)
    z4p = send(dx_send.at[2, pl.ds(0, 16)], dx_half.at[0], "z", 2)
    z4m = send(dx_send.at[2, pl.ds(16, 16)], dx_half.at[1], "z", -2)
    by_gap = dot(slope[...], oh[...], TN) + dot(slope_lo[...], oh[...], TN)
    lane_w = lax.broadcasted_iota(jnp.int32, (NW, 128), 1)
    apart = jnp.abs((lane_w % 16).astype(F32) - yg[:, D:DE].astype(F32))
    apart = jnp.where(lane_w < 16, jnp.minimum(apart, 7.0), 8.0)
    row_s = lax.broadcasted_iota(jnp.int32, (16, 128), 0)
    stats = jnp.where(row_s == 8, jnp.sum(loss_sum, axis=0, keepdims=True), 0.0)
    stats = jnp.where(row_s == 9, jnp.sum(temp_sum, axis=0, keepdims=True), stats)
    for k in range(8):
        bucket = jnp.sum(jnp.where(apart == float(k), by_gap, 0.0), axis=0, keepdims=True)
        stats = jnp.where(row_s == k, -bucket, stats)

    stat_core = share(stats, st_core, "core")
    x1_to(0, 2, True)
    x1_to(1, 4, True)
    x1_to(0, 6, False)
    x1_to(1, 0, False)
    win_grad(0, 128)
    x1_to(0, 0, True)
    x1_to(1, 6, True)
    swaps[1].wait_recv()
    swaps[2].wait_recv()
    dx_send[3] = own(1).astype(BF16)
    z1p = send(dx_send.at[3], dx_near.at[0], "z", 1)
    dx_send[4] = own(-1).astype(BF16)
    z1m = send(dx_send.at[4], dx_near.at[1], "z", -1)
    stat_y = share(summed(stat_core, st_core), st_y, "y")
    dx_mid[0] = own(2)
    dx_mid[1] = own(-2)
    swaps[3].wait_recv()

    ysent = []

    def along_y(j):
        at = slice(j * YR, (j + 1) * YR)
        part = dy[at, :] + x1_recv[0, at, :].astype(F32) + x1_recv[1, at, :].astype(F32)
        y_send[j] = part.astype(BF16)
        ysent.append(send(y_send.at[j], y_recv.at[j], "y", j))

    z3p.wait_recv()
    z4p.wait_recv()
    part = dx_mid[0] + dx_far[0].astype(F32)
    dx_send[5, 0:16] = (part[0:16] + dx_half[0].astype(F32)).astype(BF16)
    dx_send[5, 16:32] = part[16:32].astype(BF16)
    z2p = send(dx_send.at[5], dx_next.at[0], "z", 2)
    z3m.wait_recv()
    z4m.wait_recv()
    part = dx_mid[1] + dx_far[1].astype(F32)
    dx_send[6, 0:16] = part[0:16].astype(BF16)
    dx_send[6, 16:32] = (part[16:32] + dx_half[1].astype(F32)).astype(BF16)
    z2m = send(dx_send.at[6], dx_next.at[1], "z", -2)

    stat_z = share(summed(stat_y, st_y), st_z, "z")
    x1[1, 4].wait_recv()
    x1[0, 4].wait_recv()
    along_y(4)
    along_y(5)
    x1[0, 2].wait_recv()
    x1[1, 2].wait_recv()
    along_y(3)
    along_y(2)
    stat_x = share(summed(stat_z, st_z), st_x, "x")
    x1[0, 6].wait_recv()
    x1[1, 6].wait_recv()
    along_y(6)
    along_y(7)
    x1[0, 0].wait_recv()
    x1[1, 0].wait_recv()
    along_y(1)
    mine = dy[0:YR, :] + x1_recv[0, 0:YR, :].astype(F32) + x1_recv[1, 0:YR, :].astype(F32)

    temperature = jnp.exp(jnp.broadcast_to(nef_ref[...], (XR, D)))
    for copy in (z1p, z1m, z2p, z2m):
        copy.wait_recv()
    full = own(0) + dx_near[0].astype(F32) + dx_near[1].astype(F32)
    full = full + dx_next[0].astype(F32) + dx_next[1].astype(F32)
    out_ref[0:XR, :] = temperature * full

    stats = jnp.sum(summed(stat_x, st_x), axis=1, keepdims=True) * (1.0 / PAIRS)
    lane_s = lax.broadcasted_iota(jnp.int32, (8, 128), 1)
    diagonal = lax.broadcasted_iota(jnp.int32, (8, 128), 0) == lane_s
    buckets = jnp.sum(jnp.where(diagonal, stats[0:8], 0.0), axis=0, keepdims=True)
    row_s = lax.broadcasted_iota(jnp.int32, (8, 128), 0)
    out = jnp.where(row_s == 0, buckets, 0.0)
    out = jnp.where(row_s == 1, stats[8:9], out)
    out = jnp.where(row_s == 2, stats[9:10], out)
    out = jnp.where(row_s == 3, -jnp.sum(stats[0:8], axis=0, keepdims=True), out)
    out_ref[XR + YR : XR + YR + 8, 0:128] = out

    for copy in ysent:
        copy.wait_recv()
    for j in range(1, NY):
        mine = mine + y_recv[j].astype(F32)
    out_ref[XR : XR + YR, :] = temperature[0:YR] * mine

    for copy in started:
        copy.wait_send()


COPIES = 140


def finish(packed, loss, gt, gw, bias, temp, penalty):
    gt[...] = packed[0:XR, :]
    gw[...] = packed[XR : XR + YR, :].reshape(YR, 1, D)
    penalty[...] = packed[XR + YR, 0:8]
    loss[...] = packed[XR + YR + 1, 0:1]
    temp[...] = packed[XR + YR + 2, 0:1]
    bias[...] = packed[XR + YR + 3, 0:1]


def local(timelines, windows, row_gap, col_gap, positive, nef, bias, deduction):
    vmem = pl.BlockSpec(memory_space=pltpu.VMEM)
    anywhere = pl.BlockSpec(memory_space=pltpu.HBM)
    shape = jax.ShapeDtypeStruct
    packed = pl.pallas_call(
        kernel,
        out_shape=shape((XR + YR + 8, D), F32),
        in_specs=[vmem] * 2 + [anywhere] * 6,
        out_specs=vmem,
        scratch_shapes=[
            pltpu.SMEM((8,), F32),
            pltpu.VMEM((1, XR), jnp.int32),
            pltpu.VMEM((1, XR), jnp.int32),
            pltpu.VMEM((1, YR), jnp.int32),
            pltpu.VMEM((NR, DE), BF16),
            pltpu.VMEM((NW, DE), BF16),
            pltpu.VMEM((NR, 128), BF16),
            pltpu.VMEM((NW, 128), BF16),
            pltpu.VMEM((NR, NW), F32),
            pltpu.VMEM((NR, NW), F32),
            pltpu.VMEM((NR, NW), BF16),
            pltpu.VMEM((NR, NW), BF16),
            pltpu.VMEM((NR, D), F32),
            pltpu.VMEM((HALF, D), F32),
            pltpu.VMEM((7, XR, D), BF16),
            pltpu.VMEM((2, XR, D), BF16),
            pltpu.VMEM((2, 16, D), BF16),
            pltpu.VMEM((2, XR, D), BF16),
            pltpu.VMEM((2, XR, D), F32),
            pltpu.VMEM((2, XR, D), BF16),
            pltpu.VMEM((NW, D), F32),
            pltpu.VMEM((128, D), BF16),
            pltpu.VMEM((128, D), BF16),
            pltpu.VMEM((2, 128, D), BF16),
            pltpu.VMEM((2, 128, D), BF16),
            pltpu.VMEM((NY, YR, D), BF16),
            pltpu.VMEM((NY, YR, D), BF16),
            pltpu.VMEM((2, 16, 128), F32),
            pltpu.VMEM((NZ, 16, 128), F32),
            pltpu.VMEM((NY, 16, 128), F32),
            pltpu.VMEM((NX, 16, 128), F32),
            pltpu.SemaphoreType.DMA((6,)),
            pltpu.SemaphoreType.DMA((COPIES,)),
            pltpu.SemaphoreType.DMA((COPIES,)),
        ],
        compiler_params=pltpu.CompilerParams(
            collective_id=0, has_side_effects=True, vmem_limit_bytes=56 << 20
        ),
        name="loss_and_gradients",
    )(
        nef.reshape(1, 1), bias.reshape(1, 1), deduction, timelines, windows.reshape(YR, D),
        row_gap.reshape(1, XR), positive.reshape(1, XR), col_gap.reshape(1, YR),
    )
    return pl.pallas_call(
        finish,
        out_shape=(
            shape((1,), F32), shape((XR, D), F32), shape((YR, 1, D), F32),
            shape((1,), F32), shape((1,), F32), shape((8,), F32),
        ),
        in_specs=[vmem],
        out_specs=(vmem,) * 6,
        name="finish",
    )(packed)


def solution(mesh):
    return jax.shard_map(
        local,
        mesh=mesh,
        in_specs=(
            P(("row", "col"), None),
            P("row", "col", None),
            P(("row", "col")),
            P("row", "col"),
            P(("row", "col")),
            P(),
            P(),
            P(),
        ),
        out_specs=(P(), P(("row", "col"), None), P("row", "col", None), P(), P(), P()),
        check_vma=False,
    )
```

```python
import jax
import jax.numpy as jnp
from jax import lax
from jax.experimental import pallas as pl
from jax.experimental.pallas import tpu as pltpu
from jax.sharding import PartitionSpec as P

MESH = pl.DeviceIdType.MESH
F32 = jnp.float32
BF16 = jnp.bfloat16

D = 1024
DE = D + 128
XR = 32
YR = 16
NZ, NY, NX = 8, 8, 4
NR = XR * NZ * 2
NW = YR * NY * NX
HALF = NR // 2
PAIRS = 134217728
SIZES = {"core": 2, "x": NX, "y": NY, "z": NZ}
GROUP = [(axis, k) for axis in SIZES for k in range(1, SIZES[axis])]
NEAR = [(axis, k) for axis, k in GROUP if min(k, SIZES[axis] - k) <= 2]
PLACE = (0, 1, 3, 2)
NT = (((1,), (1,)), ((), ()))
TN = (((0,), (0,)), ((), ()))
NN = (((1,), (0,)), ((), ()))


def position():
    row, col = lax.axis_index("row"), lax.axis_index("col")
    return {
        "core": lax.rem(row, 2),
        "y": lax.rem(lax.div(row, 2), NY),
        "x": lax.div(row, 2 * NY) * 2 + lax.rem(col, 2),
        "z": lax.div(col, 2),
    }


def device(me, off):
    at = dict(me)
    for axis, k in off.items():
        at[axis] = lax.rem(me[axis] + (k + SIZES[axis]), SIZES[axis])
    row = lax.div(at["x"], 2) * (2 * NY) + at["y"] * 2 + at["core"]
    return (row, at["z"] * 2 + lax.rem(at["x"], 2))


def half(j):
    return 1 if 2 <= j % NY <= 5 else 0


def spot(j):
    return j % NY - 2 if half(j) else (0, 1, None, None, None, None, 2, 3)[j % NY]


def dot(a, b, dims):
    return lax.dot_general(a, b, dims, preferred_element_type=F32)


def kernel(
    nef_ref, bias_ref, ded_in, t_ref, w_ref, gap_in, pos_in, colgap_in,
    out_ref,
    ded_ref, gap_ref, pos_ref, colgap_ref,
    xg, yg, oh, pt, sim, dm, slope, slope_lo,
    dx, dx_core, dx_send, dx_far, dx_half, dx_near, dx_mid, dx_next,
    dy, x1_send, x1_recv, y_send, y_far, y_half, y_near, y_next, y_sum, x2_recv,
    st_x, st_z, st_y,
    local_sem, send_sem, recv_sem,
):
    me = position()
    ids = {(axis, k): device(me, {axis: k}) for axis, k in GROUP}
    barrier = pltpu.get_barrier_semaphore()
    for near in NEAR:
        pl.semaphore_signal(barrier, inc=1, device_id=ids[near], device_id_type=MESH)

    fetched = []
    for src, dst in (
        (gap_in, gap_ref),
        (pos_in, pos_ref),
        (colgap_in, colgap_ref),
        (w_ref, yg.at[pl.ds(0, YR), pl.ds(0, D)]),
        (t_ref, xg.at[pl.ds(0, XR), pl.ds(0, D)]),
        (ded_in, ded_ref),
    ):
        copy = pltpu.make_async_copy(src, dst, local_sem.at[len(fetched)])
        copy.start()
        fetched.append(copy)

    started = []

    def send(src, dst, axis, k):
        return send_to(src, dst, ids[axis, k % SIZES[axis]])

    def send_to(src, dst, there):
        i = len(started)
        copy = pltpu.make_async_remote_copy(
            src_ref=src,
            dst_ref=dst,
            send_sem=send_sem.at[i],
            recv_sem=recv_sem.at[i],
            device_id=there,
            device_id_type=MESH,
        )
        copy.start()
        started.append(copy)
        return copy

    for copy in fetched:
        copy.wait()
    lane = lax.broadcasted_iota(jnp.int32, (XR, 128), 1)

    def column(ref, n):
        diagonal = lax.broadcasted_iota(jnp.int32, (n, n), 0) == lax.broadcasted_iota(
            jnp.int32, (n, n), 1
        )
        row = jnp.broadcast_to(ref[...].astype(F32), (n, n))
        return jnp.sum(jnp.where(diagonal, row, 0.0), axis=1, keepdims=True)

    gap, pos = column(gap_ref, XR), column(pos_ref, XR)
    pos_high = jnp.floor(pos * (1.0 / 128.0))
    pos_low = pos - 128.0 * pos_high
    extra = jnp.where(
        lane == 0, gap, jnp.where(lane == 1, pos_high, jnp.where(lane == 2, pos_low, 0.0))
    )
    xg[0:XR, D:DE] = extra.astype(BF16)
    yg[0:YR, D:DE] = jnp.broadcast_to(column(colgap_ref, YR), (YR, 128)).astype(BF16)

    pl.semaphore_wait(barrier, len(NEAR))

    def xs(k):
        return xg.at[pl.ds((k % NZ) * XR, XR)]

    def xs_other(k):
        return xg.at[pl.ds(HALF + (k % NZ) * XR, XR)]

    def ys(i, j):
        return yg.at[pl.ds(half(j) * 256 + PLACE[i % NX] * 64 + spot(j) * YR, YR)]

    lo_cols, hi_cols = pl.ds(0, 512), pl.ds(512, DE - 512)
    xp, xm, core = {}, {}, {}

    def to_x(j):
        xp[j] = send(ys(0, j), ys(-1, j), "x", 1)
        xm[j] = send(ys(0, j), ys(1, j), "x", -1)

    def to_core(k):
        core[k] = send(xs(k), xs_other(k), "core", 1)

    x2 = send(ys(0, 0), ys(-2, 0), "x", 2)
    yp1 = send(ys(0, 0), ys(0, -1), "y", 1)
    ym1 = send(ys(0, 0), ys(0, 1), "y", -1)
    yp2 = send(ys(0, 0), ys(0, -2), "y", 2)
    ym2 = send(ys(0, 0), ys(0, 2), "y", -2)
    to_x(0)
    zp2 = send(xs(0), xs(-2), "z", 2)
    zm2 = send(xs(0), xs(2), "z", -2)
    zp1 = send(xs(0), xs(-1), "z", 1)
    zm1 = send(xs(0), xs(1), "z", -1)
    to_core(0)

    yp1.wait_recv()
    to_x(-1)
    ym1.wait_recv()
    to_x(1)
    x2.wait_recv()
    fp2 = send(ys(2, 0), ys(2, -2), "y", 2)
    fm2 = send(ys(2, 0), ys(2, 2), "y", -2)
    fp1 = send(ys(2, 0), ys(2, -1), "y", 1)
    fm1 = send(ys(2, 0), ys(2, 1), "y", -1)
    yp2.wait_recv()
    yp4 = send(ys(0, -2).at[:, lo_cols], ys(0, 4).at[:, lo_cols], "y", 2)
    yp3 = send(ys(0, -2), ys(0, -3), "y", 1)
    to_x(-2)
    ym2.wait_recv()
    ym4 = send(ys(0, 2).at[:, hi_cols], ys(0, 4).at[:, hi_cols], "y", -2)
    ym3 = send(ys(0, 2), ys(0, 3), "y", -1)
    to_x(2)
    zp2.wait_recv()
    zp4 = send(xs(-2).at[pl.ds(0, 16)], xs(4).at[pl.ds(0, 16)], "z", 2)
    zp3 = send(xs(-2), xs(-3), "z", 1)
    zm2.wait_recv()
    zm4 = send(xs(2).at[pl.ds(16, 16)], xs(4).at[pl.ds(16, 16)], "z", -2)
    zm3 = send(xs(2), xs(3), "z", -1)
    to_core(-2)
    to_core(2)
    fp2.wait_recv()
    fp4 = send(ys(2, -2).at[:, lo_cols], ys(2, 4).at[:, lo_cols], "y", 2)
    fp3 = send(ys(2, -2), ys(2, -3), "y", 1)
    fm2.wait_recv()
    fm4 = send(ys(2, 2).at[:, hi_cols], ys(2, 4).at[:, hi_cols], "y", -2)
    fm3 = send(ys(2, 2), ys(2, 3), "y", -1)
    yp3.wait_recv()
    to_x(-3)
    ym3.wait_recv()
    to_x(3)
    yp4.wait_recv()
    ym4.wait_recv()
    to_x(4)
    zp1.wait_recv()
    to_core(-1)
    zm1.wait_recv()
    to_core(1)
    zp3.wait_recv()
    to_core(-3)
    zm3.wait_recv()
    to_core(3)
    zp4.wait_recv()
    zm4.wait_recv()
    to_core(4)
    for copy in core.values():
        copy.wait_recv()
    lane = lax.broadcasted_iota(jnp.int32, (NR, 128), 1)
    lane16 = (lane % 16).astype(F32)
    gap = xg[:, D:DE].astype(F32)[:, 0:1]
    oh[...] = jnp.where((lane16 == gap) & (lane < 48), 1.0, 0.0).astype(BF16)

    def tables(lo, hi):
        lane = lax.broadcasted_iota(jnp.int32, (hi - lo, 128), 1)
        apart = jnp.abs((lane % 16).astype(F32) - yg[lo:hi, D:DE].astype(F32))
        table = jnp.full((hi - lo, 128), ded_ref[7], F32)
        for k in range(7):
            table = jnp.where(apart == float(k), ded_ref[k], table)
        table = table - jnp.broadcast_to(bias_ref[...], (hi - lo, 128))
        first = table.astype(BF16)
        rest = table - first.astype(F32)
        second = rest.astype(BF16).astype(F32)
        third = (rest - second).astype(BF16).astype(F32)
        terms = jnp.where(lane < 32, second, jnp.where(lane < 48, third, 0.0))
        pt[lo:hi, :] = jnp.where(lane < 16, first.astype(F32), terms).astype(BF16)

    def group(lo, hi, step, sums):
        n = hi - lo
        tables(lo, hi)
        sim[:, lo:hi] = dot(xg[:, 0:D], yg[lo:hi, 0:D], NT)
        dm[:, lo:hi] = dot(oh[...], pt[lo:hi, :], NT)
        scale = jnp.exp(jnp.broadcast_to(nef_ref[...], (step, n)))
        at_lane = lax.broadcasted_iota(jnp.int32, (1, n), 1) + lo
        place = at_lane % 256 // 64
        from_x = jnp.where(place == 2, 3, jnp.where(place == 3, 2, place))
        at_spot = at_lane % 64 // YR
        from_y = jnp.where(at_lane >= 256, at_spot + 2, jnp.where(at_spot < 2, at_spot, at_spot + 4))
        win_y = (from_y + me["y"]) % NY
        win_x = (from_x + me["x"]) % NX
        win_row = (win_x // 2) * (2 * NY) + win_y * 2 + me["core"]
        ordinal = (me["z"] * 2 + win_x % 2) * 512 + win_row * YR + at_lane % YR
        ordinal = ordinal.astype(F32)

        def slopes(b, sums):
            at = pl.ds(pl.multiple_of(b * step, step), step)
            loss_sum, temp_sum = sums
            s = scale * sim[at, lo:hi]
            logit = s - dm[at, lo:hi]
            mine = xg[at, D:DE].astype(F32)
            match = (mine[:, 1:2] * 128.0 + mine[:, 2:3]) == ordinal
            z = jnp.where(match, -logit, logit)
            e = jnp.exp(-jnp.abs(z))
            r = 1.0 / (1.0 + e)
            sig = jnp.where(z >= 0.0, r, e * r)
            grad = jnp.where(match, -sig, sig)
            loss = jnp.maximum(z, 0.0) + jnp.log1p(e)
            temp = grad * s
            high = grad.astype(BF16)
            slope[at, lo:hi] = high
            slope_lo[at, lo:hi] = (grad - high.astype(F32)).astype(BF16)
            for i in range(0, step, 16):
                for j in range(0, n, 128):
                    loss_sum = loss_sum + loss[i : i + 16, j : j + 128]
                    temp_sum = temp_sum + temp[i : i + 16, j : j + 128]
            return loss_sum, temp_sum

        loss_sum, temp_sum = lax.fori_loop(0, NR // step, slopes, sums)

        by_gap = dot(slope[:, lo:hi], oh[...], TN) + dot(slope_lo[:, lo:hi], oh[...], TN)
        lane = lax.broadcasted_iota(jnp.int32, (n, 128), 1)
        apart = jnp.abs((lane % 16).astype(F32) - yg[lo:hi, D:DE].astype(F32))
        apart = jnp.where(lane < 16, jnp.minimum(apart, 7.0), 8.0)
        buckets = [
            jnp.sum(jnp.where(apart == float(k), by_gap, 0.0), axis=0, keepdims=True)
            for k in range(8)
        ]
        return loss_sum, temp_sum, buckets

    zero = jnp.zeros((16, 128), F32)
    fp1.wait_recv()
    fm1.wait_recv()
    for j in (0, -1, 1, -2):
        xp[j].wait_recv()
        xm[j].wait_recv()
    loss_sum, temp_sum, first = group(0, 256, 128, (zero, zero))
    for copy in (fp3, fm3, fp4, fm4):
        copy.wait_recv()
    for j in (2, -3, 3, 4):
        xp[j].wait_recv()
        xm[j].wait_recv()
    loss_sum, temp_sum, second = group(256, 512, 128, (loss_sum, temp_sum))

    row_s = lax.broadcasted_iota(jnp.int32, (16, 128), 0)
    stats = jnp.where(row_s == 8, jnp.sum(loss_sum, axis=0, keepdims=True), 0.0)
    stats = jnp.where(row_s == 9, jnp.sum(temp_sum, axis=0, keepdims=True), stats)
    for k in range(8):
        stats = jnp.where(row_s == k, -(first[k] + second[k]), stats)

    def share(value, slots, a, b):
        here = me[a] * SIZES[b] + me[b] if b else me[a]
        slots[here] = value
        return [
            send_to(slots.at[here], slots.at[here], device(me, {a: i, b: j} if b else {a: i}))
            for j in range(SIZES[b] if b else 1)
            for i in range(SIZES[a])
            if i + j > 0
        ]

    def summed(copies, slots):
        for copy in copies:
            copy.wait_recv()
        value = slots[0]
        for k in range(1, slots.shape[0]):
            value = value + slots[k]
        return value

    stat_x = share(stats, st_x, "x", "core")

    def win_grad(lo, hi):
        dy[lo:hi, :] = dot(slope[:, lo:hi], xg[:, 0:D], TN)

    def time_grad(lo):
        dx[lo : lo + HALF, :] = dot(slope[lo : lo + HALF, :], yg[:, 0:D], NN)

    class AlongY:
        def __init__(self, tag, part):
            self.out, self.part = y_send.at[tag], part
            self.far, self.mid = y_far.at[tag], y_half.at[tag]
            self.near, self.next = y_near.at[tag], y_next.at[tag]

        def fill(self, slot, value):
            self.out[slot] = value.astype(BF16)
            return self.out.at[slot]

        def first(self):
            across = self.fill(2, self.part(4))
            self.c4 = (
                send(across.at[:, pl.ds(0, 512)], self.mid.at[0], "y", 2),
                send(across.at[:, pl.ds(512, 512)], self.mid.at[1], "y", -2),
            )
            self.c3 = (
                send(self.fill(0, self.part(3)), self.far.at[0], "y", 1),
                send(self.fill(1, self.part(5)), self.far.at[1], "y", -1),
            )

        def nearest(self):
            self.c1 = (
                send(self.fill(3, self.part(1)), self.near.at[0], "y", 1),
                send(self.fill(4, self.part(7)), self.near.at[1], "y", -1),
            )

        def second(self):
            self.c2 = []
            for side, j in ((0, 2), (1, 6)):
                self.c3[side].wait_recv()
                self.c4[side].wait_recv()
                value = self.part(j) + self.far[side].astype(F32)
                low, high = value[:, 0:512], value[:, 512:1024]
                passing = self.mid[side].astype(F32)
                if side == 0:
                    low = low + passing
                else:
                    high = high + passing
                self.out[5 + side, :, 0:512] = low.astype(BF16)
                self.out[5 + side, :, 512:1024] = high.astype(BF16)
                self.c2.append(
                    send(self.out.at[5 + side], self.next.at[side], "y", 2 if side == 0 else -2)
                )

        def total(self):
            for copy in (*self.c1, *self.c2):
                copy.wait_recv()
            value = self.part(0)
            for arrived in (self.near, self.next):
                value = value + arrived[0].astype(F32) + arrived[1].astype(F32)
            return value

    def start(j, block):
        return half(j) * 256 + block * 64 + spot(j) * YR

    def two_away(j):
        return dy[start(j, 3) : start(j, 3) + YR, :]

    def own_column(j):
        q = spot(j) * YR
        value = dy[start(j, 0) : start(j, 0) + YR, :]
        for side in (0, 1):
            value = value + x1_recv[side, half(j), q : q + YR, :].astype(F32)
        return value

    x1 = {}

    def x1_to(h):
        for side, k in ((0, 1), (1, -1)):
            lo = h * 256 + 64 + side * 64
            x1_send[side, h] = dy[lo : lo + 64, :].astype(BF16)
            x1[side, h] = send(x1_send.at[side, h], x1_recv.at[side, h], "x", k)

    passing, column = AlongY(0, two_away), AlongY(1, own_column)
    win_grad(256, 512)
    passing.first()
    x1_to(1)

    time_grad(HALF)
    swaps = []
    for lo, n in ((3, 3), (6, 2), (0, 3)):
        at, to = pl.ds(HALF + lo * XR, n * XR), pl.ds(lo * XR, n * XR)
        swaps.append(send(dx.at[at], dx_core.at[to], "core", 1))
    win_grad(0, 256)
    x1_to(0)
    passing.nearest()
    time_grad(0)

    def own(k):
        at = pl.ds((k % NZ) * XR, XR)
        return dx[at, :] + dx_core[at, :]

    swaps[0].wait_recv()
    dx_send[2] = own(4).astype(BF16)
    z4p = send(dx_send.at[2, pl.ds(0, 16)], dx_half.at[0], "z", 2)
    z4m = send(dx_send.at[2, pl.ds(16, 16)], dx_half.at[1], "z", -2)
    dx_send[0] = own(3).astype(BF16)
    z3p = send(dx_send.at[0], dx_far.at[0], "z", 1)
    dx_send[1] = own(-3).astype(BF16)
    z3m = send(dx_send.at[1], dx_far.at[1], "z", -1)
    stat_z = share(summed(stat_x, st_x), st_z, "z", None)
    swaps[1].wait_recv()
    swaps[2].wait_recv()
    dx_send[3] = own(1).astype(BF16)
    z1p = send(dx_send.at[3], dx_near.at[0], "z", 1)
    dx_send[4] = own(-1).astype(BF16)
    z1m = send(dx_send.at[4], dx_near.at[1], "z", -1)
    dx_mid[0] = own(2)
    dx_mid[1] = own(-2)
    passing.second()
    x1[0, 1].wait_recv()
    x1[1, 1].wait_recv()
    column.first()

    z3p.wait_recv()
    z4p.wait_recv()
    part = dx_mid[0] + dx_far[0].astype(F32)
    dx_send[5, 0:16] = (part[0:16] + dx_half[0].astype(F32)).astype(BF16)
    dx_send[5, 16:32] = part[16:32].astype(BF16)
    z2p = send(dx_send.at[5], dx_next.at[0], "z", 2)
    z3m.wait_recv()
    z4m.wait_recv()
    part = dx_mid[1] + dx_far[1].astype(F32)
    dx_send[6, 0:16] = part[0:16].astype(BF16)
    dx_send[6, 16:32] = (part[16:32] + dx_half[1].astype(F32)).astype(BF16)
    z2m = send(dx_send.at[6], dx_next.at[1], "z", -2)

    x1[0, 0].wait_recv()
    x1[1, 0].wait_recv()
    column.nearest()
    y_sum[...] = passing.total()
    x2_done = send(y_sum, x2_recv, "x", 2)
    stat_y = share(summed(stat_z, st_z), st_y, "y", None)
    column.second()

    temperature = jnp.exp(jnp.broadcast_to(nef_ref[...], (XR, D)))
    for copy in (z1p, z1m, z2p, z2m):
        copy.wait_recv()
    full = own(0) + dx_near[0].astype(F32) + dx_near[1].astype(F32)
    full = full + dx_next[0].astype(F32) + dx_next[1].astype(F32)
    out_ref[0:XR, :] = temperature * full

    stats = jnp.sum(summed(stat_y, st_y), axis=1, keepdims=True) * (1.0 / PAIRS)
    lane_s = lax.broadcasted_iota(jnp.int32, (8, 128), 1)
    diagonal = lax.broadcasted_iota(jnp.int32, (8, 128), 0) == lane_s
    buckets = jnp.sum(jnp.where(diagonal, stats[0:8], 0.0), axis=0, keepdims=True)
    row_s = lax.broadcasted_iota(jnp.int32, (8, 128), 0)
    out = jnp.where(row_s == 0, buckets, 0.0)
    out = jnp.where(row_s == 1, stats[8:9], out)
    out = jnp.where(row_s == 2, stats[9:10], out)
    out = jnp.where(row_s == 3, -jnp.sum(stats[0:8], axis=0, keepdims=True), out)
    out_ref[XR + YR : XR + YR + 8, 0:128] = out

    mine = column.total()
    x2_done.wait_recv()
    mine = mine + x2_recv[...]
    out_ref[XR : XR + YR, :] = temperature[0:YR] * mine

    for copy in started:
        copy.wait_send()


COPIES = 192


def finish(packed, loss, gt, gw, bias, temp, penalty):
    gt[...] = packed[0:XR, :]
    gw[...] = packed[XR : XR + YR, :].reshape(YR, 1, D)
    penalty[...] = packed[XR + YR, 0:8]
    loss[...] = packed[XR + YR + 1, 0:1]
    temp[...] = packed[XR + YR + 2, 0:1]
    bias[...] = packed[XR + YR + 3, 0:1]


def local(timelines, windows, row_gap, col_gap, positive, nef, bias, deduction):
    vmem = pl.BlockSpec(memory_space=pltpu.VMEM)
    anywhere = pl.BlockSpec(memory_space=pltpu.HBM)
    shape = jax.ShapeDtypeStruct
    packed = pl.pallas_call(
        kernel,
        out_shape=shape((XR + YR + 8, D), F32),
        in_specs=[vmem] * 2 + [anywhere] * 6,
        out_specs=vmem,
        scratch_shapes=[
            pltpu.SMEM((8,), F32),
            pltpu.VMEM((1, XR), jnp.int32),
            pltpu.VMEM((1, XR), jnp.int32),
            pltpu.VMEM((1, YR), jnp.int32),
            pltpu.VMEM((NR, DE), BF16),
            pltpu.VMEM((NW, DE), BF16),
            pltpu.VMEM((NR, 128), BF16),
            pltpu.VMEM((NW, 128), BF16),
            pltpu.VMEM((NR, NW), F32),
            pltpu.VMEM((NR, NW), F32),
            pltpu.VMEM((NR, NW), BF16),
            pltpu.VMEM((NR, NW), BF16),
            pltpu.VMEM((NR, D), F32),
            pltpu.VMEM((HALF, D), F32),
            pltpu.VMEM((7, XR, D), BF16),
            pltpu.VMEM((2, XR, D), BF16),
            pltpu.VMEM((2, 16, D), BF16),
            pltpu.VMEM((2, XR, D), BF16),
            pltpu.VMEM((2, XR, D), F32),
            pltpu.VMEM((2, XR, D), BF16),
            pltpu.VMEM((NW, D), F32),
            pltpu.VMEM((2, 2, 64, D), BF16),
            pltpu.VMEM((2, 2, 64, D), BF16),
            pltpu.VMEM((2, 7, YR, D), BF16),
            pltpu.VMEM((2, 2, YR, D), BF16),
            pltpu.VMEM((2, 2, YR, 512), BF16),
            pltpu.VMEM((2, 2, YR, D), BF16),
            pltpu.VMEM((2, 2, YR, D), BF16),
            pltpu.VMEM((YR, D), F32),
            pltpu.VMEM((YR, D), F32),
            pltpu.VMEM((NX * 2, 16, 128), F32),
            pltpu.VMEM((NZ, 16, 128), F32),
            pltpu.VMEM((NY, 16, 128), F32),
            pltpu.SemaphoreType.DMA((6,)),
            pltpu.SemaphoreType.DMA((COPIES,)),
            pltpu.SemaphoreType.DMA((COPIES,)),
        ],
        compiler_params=pltpu.CompilerParams(
            collective_id=0, has_side_effects=True, vmem_limit_bytes=56 << 20
        ),
        name="loss_and_gradients",
    )(
        nef.reshape(1, 1), bias.reshape(1, 1), deduction, timelines, windows.reshape(YR, D),
        row_gap.reshape(1, XR), positive.reshape(1, XR), col_gap.reshape(1, YR),
    )
    return pl.pallas_call(
        finish,
        out_shape=(
            shape((1,), F32), shape((XR, D), F32), shape((YR, 1, D), F32),
            shape((1,), F32), shape((1,), F32), shape((8,), F32),
        ),
        in_specs=[vmem],
        out_specs=(vmem,) * 6,
        name="finish",
    )(packed)


def solution(mesh):
    return jax.shard_map(
        local,
        mesh=mesh,
        in_specs=(
            P(("row", "col"), None),
            P("row", "col", None),
            P(("row", "col")),
            P("row", "col"),
            P(("row", "col")),
            P(),
            P(),
            P(),
        ),
        out_specs=(P(), P(("row", "col"), None), P("row", "col", None), P(), P(), P()),
        check_vma=False,
    )
```

```python
import jax
import jax.numpy as jnp
from jax import lax
from jax.experimental import pallas as pl
from jax.experimental.pallas import tpu as pltpu
from jax.sharding import PartitionSpec as P

MESH = pl.DeviceIdType.MESH
F32 = jnp.float32
BF16 = jnp.bfloat16

D = 1024
DE = D + 128
XR = 32
YR = 16
NZ, NY, NX = 8, 8, 4
NR = XR * NZ * 2
NW = YR * NY * NX
HALF = NR // 2
PAIRS = 134217728
SIZES = {"core": 2, "x": NX, "y": NY, "z": NZ}
GROUP = [(axis, k) for axis in SIZES for k in range(1, SIZES[axis])]
NEAR = [(axis, k) for axis, k in GROUP if min(k, SIZES[axis] - k) <= 2]
PLACE = (0, 1, 3, 2)
NT = (((1,), (1,)), ((), ()))
TN = (((0,), (0,)), ((), ()))
NN = (((1,), (0,)), ((), ()))


def position():
    row, col = lax.axis_index("row"), lax.axis_index("col")
    return {
        "core": lax.rem(row, 2),
        "y": lax.rem(lax.div(row, 2), NY),
        "x": lax.div(row, 2 * NY) * 2 + lax.rem(col, 2),
        "z": lax.div(col, 2),
    }


def device(me, off):
    at = dict(me)
    for axis, k in off.items():
        at[axis] = lax.rem(me[axis] + (k + SIZES[axis]), SIZES[axis])
    row = lax.div(at["x"], 2) * (2 * NY) + at["y"] * 2 + at["core"]
    return (row, at["z"] * 2 + lax.rem(at["x"], 2))


def half(j):
    return 1 if 2 <= j % NY <= 5 else 0


def spot(j):
    return j % NY - 2 if half(j) else (0, 1, None, None, None, None, 2, 3)[j % NY]


def dot(a, b, dims):
    return lax.dot_general(a, b, dims, preferred_element_type=F32)


def kernel(
    nef_ref, bias_ref, ded_in, t_ref, w_ref, gap_in, pos_in, colgap_in,
    out_ref,
    ded_ref, gap_ref, pos_ref, colgap_ref,
    xg, yg, oh, pt, sim, dm, slope, slope_lo,
    dx, dx_core, dx_send, dx_far, dx_half, dx_near, dx_mid, dx_next,
    dy, x1_send, x1_recv, y_send, y_far, y_half, y_near, y_next, y_sum, x2_recv,
    st_x, st_z, st_y,
    local_sem, send_sem, recv_sem,
):
    me = position()
    ids = {(axis, k): device(me, {axis: k}) for axis, k in GROUP}
    barrier = pltpu.get_barrier_semaphore()
    for near in NEAR:
        pl.semaphore_signal(barrier, inc=1, device_id=ids[near], device_id_type=MESH)

    fetched = []
    for src, dst in (
        (gap_in, gap_ref),
        (pos_in, pos_ref),
        (colgap_in, colgap_ref),
        (w_ref, yg.at[pl.ds(0, YR), pl.ds(0, D)]),
        (t_ref, xg.at[pl.ds(0, XR), pl.ds(0, D)]),
        (ded_in, ded_ref),
    ):
        copy = pltpu.make_async_copy(src, dst, local_sem.at[len(fetched)])
        copy.start()
        fetched.append(copy)

    started = []

    def send(src, dst, axis, k):
        return send_to(src, dst, ids[axis, k % SIZES[axis]])

    def send_to(src, dst, there):
        i = len(started)
        copy = pltpu.make_async_remote_copy(
            src_ref=src,
            dst_ref=dst,
            send_sem=send_sem.at[i],
            recv_sem=recv_sem.at[i],
            device_id=there,
            device_id_type=MESH,
        )
        copy.start()
        started.append(copy)
        return copy

    for copy in fetched:
        copy.wait()
    lane = lax.broadcasted_iota(jnp.int32, (XR, 128), 1)

    def column(ref, n):
        diagonal = lax.broadcasted_iota(jnp.int32, (n, n), 0) == lax.broadcasted_iota(
            jnp.int32, (n, n), 1
        )
        row = jnp.broadcast_to(ref[...].astype(F32), (n, n))
        return jnp.sum(jnp.where(diagonal, row, 0.0), axis=1, keepdims=True)

    gap, pos = column(gap_ref, XR), column(pos_ref, XR)
    pos_high = jnp.floor(pos * (1.0 / 128.0))
    pos_low = pos - 128.0 * pos_high
    extra = jnp.where(
        lane == 0, gap, jnp.where(lane == 1, pos_high, jnp.where(lane == 2, pos_low, 0.0))
    )
    xg[0:XR, D:DE] = extra.astype(BF16)
    yg[0:YR, D:DE] = jnp.broadcast_to(column(colgap_ref, YR), (YR, 128)).astype(BF16)

    pl.semaphore_wait(barrier, len(NEAR))

    def xs(k):
        return xg.at[pl.ds((k % NZ) * XR, XR)]

    def xs_other(k):
        return xg.at[pl.ds(HALF + (k % NZ) * XR, XR)]

    def ys(i, j):
        return yg.at[pl.ds(half(j) * 256 + PLACE[i % NX] * 64 + spot(j) * YR, YR)]

    lo_cols, hi_cols = pl.ds(0, 512), pl.ds(512, DE - 512)
    xp, xm, core = {}, {}, {}

    def to_x(j):
        xp[j] = send(ys(0, j), ys(-1, j), "x", 1)
        xm[j] = send(ys(0, j), ys(1, j), "x", -1)

    def to_core(k):
        core[k] = send(xs(k), xs_other(k), "core", 1)

    x2 = send(ys(0, 0), ys(-2, 0), "x", 2)
    yp1 = send(ys(0, 0), ys(0, -1), "y", 1)
    ym1 = send(ys(0, 0), ys(0, 1), "y", -1)
    yp2 = send(ys(0, 0), ys(0, -2), "y", 2)
    ym2 = send(ys(0, 0), ys(0, 2), "y", -2)
    to_x(0)
    zp2 = send(xs(0), xs(-2), "z", 2)
    zm2 = send(xs(0), xs(2), "z", -2)
    zp1 = send(xs(0), xs(-1), "z", 1)
    zm1 = send(xs(0), xs(1), "z", -1)
    to_core(0)

    yp1.wait_recv()
    to_x(-1)
    ym1.wait_recv()
    to_x(1)
    x2.wait_recv()
    fp2 = send(ys(2, 0), ys(2, -2), "y", 2)
    fm2 = send(ys(2, 0), ys(2, 2), "y", -2)
    yp2.wait_recv()
    yp4 = send(ys(0, -2).at[:, lo_cols], ys(0, 4).at[:, lo_cols], "y", 2)
    yp3 = send(ys(0, -2), ys(0, -3), "y", 1)
    to_x(-2)
    ym2.wait_recv()
    ym4 = send(ys(0, 2).at[:, hi_cols], ys(0, 4).at[:, hi_cols], "y", -2)
    ym3 = send(ys(0, 2), ys(0, 3), "y", -1)
    fp1 = send(ys(2, 0), ys(2, -1), "y", 1)
    fm1 = send(ys(2, 0), ys(2, 1), "y", -1)
    to_x(2)
    zp2.wait_recv()
    zp4 = send(xs(-2).at[pl.ds(0, 16)], xs(4).at[pl.ds(0, 16)], "z", 2)
    zp3 = send(xs(-2), xs(-3), "z", 1)
    zm2.wait_recv()
    zm4 = send(xs(2).at[pl.ds(16, 16)], xs(4).at[pl.ds(16, 16)], "z", -2)
    zm3 = send(xs(2), xs(3), "z", -1)
    to_core(-2)
    to_core(2)
    fp2.wait_recv()
    fp4 = send(ys(2, -2).at[:, lo_cols], ys(2, 4).at[:, lo_cols], "y", 2)
    fp3 = send(ys(2, -2), ys(2, -3), "y", 1)
    fm2.wait_recv()
    fm4 = send(ys(2, 2).at[:, hi_cols], ys(2, 4).at[:, hi_cols], "y", -2)
    fm3 = send(ys(2, 2), ys(2, 3), "y", -1)
    yp3.wait_recv()
    to_x(-3)
    ym3.wait_recv()
    to_x(3)
    yp4.wait_recv()
    ym4.wait_recv()
    to_x(4)
    zp1.wait_recv()
    to_core(-1)
    zm1.wait_recv()
    to_core(1)
    zp3.wait_recv()
    to_core(-3)
    zm3.wait_recv()
    to_core(3)
    zp4.wait_recv()
    zm4.wait_recv()
    to_core(4)
    for copy in core.values():
        copy.wait_recv()
    lane = lax.broadcasted_iota(jnp.int32, (NR, 128), 1)
    lane16 = (lane % 16).astype(F32)
    gap = xg[:, D:DE].astype(F32)[:, 0:1]
    oh[...] = jnp.where((lane16 == gap) & (lane < 48), 1.0, 0.0).astype(BF16)

    def tables(lo, hi):
        lane = lax.broadcasted_iota(jnp.int32, (hi - lo, 128), 1)
        apart = jnp.abs((lane % 16).astype(F32) - yg[lo:hi, D:DE].astype(F32))
        table = jnp.full((hi - lo, 128), ded_ref[7], F32)
        for k in range(7):
            table = jnp.where(apart == float(k), ded_ref[k], table)
        table = table - jnp.broadcast_to(bias_ref[...], (hi - lo, 128))
        first = table.astype(BF16)
        rest = table - first.astype(F32)
        second = rest.astype(BF16).astype(F32)
        third = (rest - second).astype(BF16).astype(F32)
        terms = jnp.where(lane < 32, second, jnp.where(lane < 48, third, 0.0))
        pt[lo:hi, :] = jnp.where(lane < 16, first.astype(F32), terms).astype(BF16)

    def group(lo, hi, step, sums):
        n = hi - lo
        tables(lo, hi)
        sim[:, lo:hi] = dot(xg[:, 0:D], yg[lo:hi, 0:D], NT)
        dm[:, lo:hi] = dot(oh[...], pt[lo:hi, :], NT)
        scale = jnp.exp(jnp.broadcast_to(nef_ref[...], (step, n)))
        at_lane = lax.broadcasted_iota(jnp.int32, (1, n), 1) + lo
        place = at_lane % 256 // 64
        from_x = jnp.where(place == 2, 3, jnp.where(place == 3, 2, place))
        at_spot = at_lane % 64 // YR
        from_y = jnp.where(at_lane >= 256, at_spot + 2, jnp.where(at_spot < 2, at_spot, at_spot + 4))
        win_y = (from_y + me["y"]) % NY
        win_x = (from_x + me["x"]) % NX
        win_row = (win_x // 2) * (2 * NY) + win_y * 2 + me["core"]
        ordinal = (me["z"] * 2 + win_x % 2) * 512 + win_row * YR + at_lane % YR
        ordinal = ordinal.astype(F32)

        def slopes(b, sums):
            at = pl.ds(b * step if step == NR else pl.multiple_of(b * step, step), step)
            loss_sum, temp_sum = sums
            s = scale * sim[at, lo:hi]
            logit = s - dm[at, lo:hi]
            mine = xg[at, D:DE].astype(F32)
            match = (mine[:, 1:2] * 128.0 + mine[:, 2:3]) == ordinal
            z = jnp.where(match, -logit, logit)
            e = jnp.exp(-jnp.abs(z))
            r = 1.0 / (1.0 + e)
            sig = jnp.where(z >= 0.0, r, e * r)
            grad = jnp.where(match, -sig, sig)
            loss = jnp.maximum(z, 0.0) + jnp.log1p(e)
            temp = grad * s
            high = grad.astype(BF16)
            slope[at, lo:hi] = high
            slope_lo[at, lo:hi] = (grad - high.astype(F32)).astype(BF16)
            for i in range(0, step, 16):
                for j in range(0, n, 128):
                    loss_sum = loss_sum + loss[i : i + 16, j : j + 128]
                    temp_sum = temp_sum + temp[i : i + 16, j : j + 128]
            return loss_sum, temp_sum

        if step == NR:
            loss_sum, temp_sum = slopes(0, sums)
        else:
            loss_sum, temp_sum = lax.fori_loop(0, NR // step, slopes, sums)

        by_gap = dot(slope[:, lo:hi], oh[...], TN) + dot(slope_lo[:, lo:hi], oh[...], TN)
        lane = lax.broadcasted_iota(jnp.int32, (n, 128), 1)
        apart = jnp.abs((lane % 16).astype(F32) - yg[lo:hi, D:DE].astype(F32))
        apart = jnp.where(lane < 16, jnp.minimum(apart, 7.0), 8.0)
        buckets = [
            jnp.sum(jnp.where(apart == float(k), by_gap, 0.0), axis=0, keepdims=True)
            for k in range(8)
        ]
        return loss_sum, temp_sum, buckets

    zero = jnp.zeros((16, 128), F32)
    fp1.wait_recv()
    fm1.wait_recv()
    for j in (0, -1, 1, -2):
        xp[j].wait_recv()
        xm[j].wait_recv()
    loss_sum, temp_sum, first = group(0, 256, 128, (zero, zero))
    for copy in (fp3, fm3, fp4, fm4):
        copy.wait_recv()
    for j in (2, -3, 3, 4):
        xp[j].wait_recv()
        xm[j].wait_recv()
    loss_sum, temp_sum, second = group(256, 512, NR, (loss_sum, temp_sum))

    row_s = lax.broadcasted_iota(jnp.int32, (16, 128), 0)
    stats = jnp.where(row_s == 8, jnp.sum(loss_sum, axis=0, keepdims=True), 0.0)
    stats = jnp.where(row_s == 9, jnp.sum(temp_sum, axis=0, keepdims=True), stats)
    for k in range(8):
        stats = jnp.where(row_s == k, -(first[k] + second[k]), stats)

    def share(value, slots, a, b):
        here = me[a] * SIZES[b] + me[b] if b else me[a]
        slots[here] = value
        return [
            send_to(slots.at[here], slots.at[here], device(me, {a: i, b: j} if b else {a: i}))
            for j in range(SIZES[b] if b else 1)
            for i in range(SIZES[a])
            if i + j > 0
        ]

    def summed(copies, slots):
        for copy in copies:
            copy.wait_recv()
        value = slots[0]
        for k in range(1, slots.shape[0]):
            value = value + slots[k]
        return value

    stat_x = share(stats, st_x, "x", "core")

    def win_grad(lo, hi):
        dy[lo:hi, :] = dot(slope[:, lo:hi], xg[:, 0:D], TN)

    def time_grad(lo):
        dx[lo : lo + HALF, :] = dot(slope[lo : lo + HALF, :], yg[:, 0:D], NN)

    class AlongY:
        def __init__(self, tag, part):
            self.out, self.part = y_send.at[tag], part
            self.far, self.mid = y_far.at[tag], y_half.at[tag]
            self.near, self.next = y_near.at[tag], y_next.at[tag]

        def fill(self, slot, value):
            self.out[slot] = value.astype(BF16)
            return self.out.at[slot]

        def first(self):
            across = self.fill(2, self.part(4))
            self.c4 = (
                send(across.at[:, pl.ds(0, 512)], self.mid.at[0], "y", 2),
                send(across.at[:, pl.ds(512, 512)], self.mid.at[1], "y", -2),
            )
            self.c3 = (
                send(self.fill(0, self.part(3)), self.far.at[0], "y", 1),
                send(self.fill(1, self.part(5)), self.far.at[1], "y", -1),
            )

        def nearest(self):
            self.c1 = (
                send(self.fill(3, self.part(1)), self.near.at[0], "y", 1),
                send(self.fill(4, self.part(7)), self.near.at[1], "y", -1),
            )

        def second(self):
            self.c2 = []
            for side, j in ((0, 2), (1, 6)):
                self.c3[side].wait_recv()
                self.c4[side].wait_recv()
                value = self.part(j) + self.far[side].astype(F32)
                low, high = value[:, 0:512], value[:, 512:1024]
                passing = self.mid[side].astype(F32)
                if side == 0:
                    low = low + passing
                else:
                    high = high + passing
                self.out[5 + side, :, 0:512] = low.astype(BF16)
                self.out[5 + side, :, 512:1024] = high.astype(BF16)
                self.c2.append(
                    send(self.out.at[5 + side], self.next.at[side], "y", 2 if side == 0 else -2)
                )

        def total(self):
            for copy in (*self.c1, *self.c2):
                copy.wait_recv()
            value = self.part(0)
            for arrived in (self.near, self.next):
                value = value + arrived[0].astype(F32) + arrived[1].astype(F32)
            return value

    def start(j, block):
        return half(j) * 256 + block * 64 + spot(j) * YR

    def two_away(j):
        return dy[start(j, 3) : start(j, 3) + YR, :]

    def own_column(j):
        q = spot(j) * YR
        value = dy[start(j, 0) : start(j, 0) + YR, :]
        for side in (0, 1):
            value = value + x1_recv[side, half(j), q : q + YR, :].astype(F32)
        return value

    x1 = {}

    def x1_to(h):
        for side, k in ((0, 1), (1, -1)):
            lo = h * 256 + 64 + side * 64
            x1_send[side, h] = dy[lo : lo + 64, :].astype(BF16)
            x1[side, h] = send(x1_send.at[side, h], x1_recv.at[side, h], "x", k)

    passing, column = AlongY(0, two_away), AlongY(1, own_column)
    win_grad(256, 512)
    passing.first()
    x1_to(1)

    time_grad(HALF)
    swaps = []
    for lo, n in ((3, 3), (6, 2), (0, 3)):
        at, to = pl.ds(HALF + lo * XR, n * XR), pl.ds(lo * XR, n * XR)
        swaps.append(send(dx.at[at], dx_core.at[to], "core", 1))
    win_grad(0, 256)
    x1_to(0)
    passing.nearest()
    time_grad(0)

    def own(k):
        at = pl.ds((k % NZ) * XR, XR)
        return dx[at, :] + dx_core[at, :]

    swaps[0].wait_recv()
    dx_send[2] = own(4).astype(BF16)
    z4p = send(dx_send.at[2, pl.ds(0, 16)], dx_half.at[0], "z", 2)
    z4m = send(dx_send.at[2, pl.ds(16, 16)], dx_half.at[1], "z", -2)
    dx_send[0] = own(3).astype(BF16)
    z3p = send(dx_send.at[0], dx_far.at[0], "z", 1)
    dx_send[1] = own(-3).astype(BF16)
    z3m = send(dx_send.at[1], dx_far.at[1], "z", -1)
    stat_y = share(summed(stat_x, st_x), st_y, "y", None)
    swaps[1].wait_recv()
    swaps[2].wait_recv()
    dx_send[3] = own(1).astype(BF16)
    z1p = send(dx_send.at[3], dx_near.at[0], "z", 1)
    dx_send[4] = own(-1).astype(BF16)
    z1m = send(dx_send.at[4], dx_near.at[1], "z", -1)
    dx_mid[0] = own(2)
    dx_mid[1] = own(-2)
    passing.second()
    x1[0, 1].wait_recv()
    x1[1, 1].wait_recv()
    column.first()

    z3p.wait_recv()
    z4p.wait_recv()
    part = dx_mid[0] + dx_far[0].astype(F32)
    dx_send[5, 0:16] = (part[0:16] + dx_half[0].astype(F32)).astype(BF16)
    dx_send[5, 16:32] = part[16:32].astype(BF16)
    z2p = send(dx_send.at[5], dx_next.at[0], "z", 2)
    z3m.wait_recv()
    z4m.wait_recv()
    part = dx_mid[1] + dx_far[1].astype(F32)
    dx_send[6, 0:16] = part[0:16].astype(BF16)
    dx_send[6, 16:32] = (part[16:32] + dx_half[1].astype(F32)).astype(BF16)
    z2m = send(dx_send.at[6], dx_next.at[1], "z", -2)

    x1[0, 0].wait_recv()
    x1[1, 0].wait_recv()
    column.nearest()
    y_sum[...] = passing.total()
    x2_done = send(y_sum, x2_recv, "x", 2)
    stat_z = share(summed(stat_y, st_y), st_z, "z", None)
    column.second()

    temperature = jnp.exp(jnp.broadcast_to(nef_ref[...], (XR, D)))
    for copy in (z1p, z1m, z2p, z2m):
        copy.wait_recv()
    full = own(0) + dx_near[0].astype(F32) + dx_near[1].astype(F32)
    full = full + dx_next[0].astype(F32) + dx_next[1].astype(F32)
    out_ref[0:XR, :] = temperature * full

    stats = jnp.sum(summed(stat_z, st_z), axis=1, keepdims=True) * (1.0 / PAIRS)
    lane_s = lax.broadcasted_iota(jnp.int32, (8, 128), 1)
    diagonal = lax.broadcasted_iota(jnp.int32, (8, 128), 0) == lane_s
    buckets = jnp.sum(jnp.where(diagonal, stats[0:8], 0.0), axis=0, keepdims=True)
    row_s = lax.broadcasted_iota(jnp.int32, (8, 128), 0)
    out = jnp.where(row_s == 0, buckets, 0.0)
    out = jnp.where(row_s == 1, stats[8:9], out)
    out = jnp.where(row_s == 2, stats[9:10], out)
    out = jnp.where(row_s == 3, -jnp.sum(stats[0:8], axis=0, keepdims=True), out)
    out_ref[XR + YR : XR + YR + 8, 0:128] = out

    mine = column.total()
    x2_done.wait_recv()
    mine = mine + x2_recv[...]
    out_ref[XR : XR + YR, :] = temperature[0:YR] * mine

    for copy in started:
        copy.wait_send()


COPIES = 192


def finish(packed, loss, gt, gw, bias, temp, penalty):
    gt[...] = packed[0:XR, :]
    gw[...] = packed[XR : XR + YR, :].reshape(YR, 1, D)
    penalty[...] = packed[XR + YR, 0:8]
    loss[...] = packed[XR + YR + 1, 0:1]
    temp[...] = packed[XR + YR + 2, 0:1]
    bias[...] = packed[XR + YR + 3, 0:1]


def local(timelines, windows, row_gap, col_gap, positive, nef, bias, deduction):
    vmem = pl.BlockSpec(memory_space=pltpu.VMEM)
    anywhere = pl.BlockSpec(memory_space=pltpu.HBM)
    shape = jax.ShapeDtypeStruct
    packed = pl.pallas_call(
        kernel,
        out_shape=shape((XR + YR + 8, D), F32),
        in_specs=[vmem] * 2 + [anywhere] * 6,
        out_specs=vmem,
        scratch_shapes=[
            pltpu.SMEM((8,), F32),
            pltpu.VMEM((1, XR), jnp.int32),
            pltpu.VMEM((1, XR), jnp.int32),
            pltpu.VMEM((1, YR), jnp.int32),
            pltpu.VMEM((NR, DE), BF16),
            pltpu.VMEM((NW, DE), BF16),
            pltpu.VMEM((NR, 128), BF16),
            pltpu.VMEM((NW, 128), BF16),
            pltpu.VMEM((NR, NW), F32),
            pltpu.VMEM((NR, NW), F32),
            pltpu.VMEM((NR, NW), BF16),
            pltpu.VMEM((NR, NW), BF16),
            pltpu.VMEM((NR, D), F32),
            pltpu.VMEM((HALF, D), F32),
            pltpu.VMEM((7, XR, D), BF16),
            pltpu.VMEM((2, XR, D), BF16),
            pltpu.VMEM((2, 16, D), BF16),
            pltpu.VMEM((2, XR, D), BF16),
            pltpu.VMEM((2, XR, D), F32),
            pltpu.VMEM((2, XR, D), BF16),
            pltpu.VMEM((NW, D), F32),
            pltpu.VMEM((2, 2, 64, D), BF16),
            pltpu.VMEM((2, 2, 64, D), BF16),
            pltpu.VMEM((2, 7, YR, D), BF16),
            pltpu.VMEM((2, 2, YR, D), BF16),
            pltpu.VMEM((2, 2, YR, 512), BF16),
            pltpu.VMEM((2, 2, YR, D), BF16),
            pltpu.VMEM((2, 2, YR, D), BF16),
            pltpu.VMEM((YR, D), F32),
            pltpu.VMEM((YR, D), F32),
            pltpu.VMEM((NX * 2, 16, 128), F32),
            pltpu.VMEM((NZ, 16, 128), F32),
            pltpu.VMEM((NY, 16, 128), F32),
            pltpu.SemaphoreType.DMA((6,)),
            pltpu.SemaphoreType.DMA((COPIES,)),
            pltpu.SemaphoreType.DMA((COPIES,)),
        ],
        compiler_params=pltpu.CompilerParams(
            collective_id=0, has_side_effects=True, vmem_limit_bytes=56 << 20
        ),
        name="loss_and_gradients",
    )(
        nef.reshape(1, 1), bias.reshape(1, 1), deduction, timelines, windows.reshape(YR, D),
        row_gap.reshape(1, XR), positive.reshape(1, XR), col_gap.reshape(1, YR),
    )
    return pl.pallas_call(
        finish,
        out_shape=(
            shape((1,), F32), shape((XR, D), F32), shape((YR, 1, D), F32),
            shape((1,), F32), shape((1,), F32), shape((8,), F32),
        ),
        in_specs=[vmem],
        out_specs=(vmem,) * 6,
        name="finish",
    )(packed)


def solution(mesh):
    return jax.shard_map(
        local,
        mesh=mesh,
        in_specs=(
            P(("row", "col"), None),
            P("row", "col", None),
            P(("row", "col")),
            P("row", "col"),
            P(("row", "col")),
            P(),
            P(),
            P(),
        ),
        out_specs=(P(), P(("row", "col"), None), P("row", "col", None), P(), P(), P()),
        check_vma=False,
    )
```

```python
import jax
import jax.numpy as jnp
from jax import lax
from jax.experimental import pallas as pl
from jax.experimental.pallas import tpu as pltpu
from jax.sharding import PartitionSpec as P

MESH = pl.DeviceIdType.MESH
F32 = jnp.float32
BF16 = jnp.bfloat16

D = 1024
DE = D + 128
XR = 32
YR = 16
NZ, NY, NX = 8, 8, 4
NR = XR * NZ * 2
NW = YR * NY * NX
HALF = NR // 2
PAIRS = 134217728
SIZES = {"core": 2, "x": NX, "y": NY, "z": NZ}
GROUP = [(axis, k) for axis in SIZES for k in range(1, SIZES[axis])]
NEAR = [(axis, k) for axis, k in GROUP if min(k, SIZES[axis] - k) <= 2]
PLACE = (0, 1, 3, 2)
NT = (((1,), (1,)), ((), ()))
TN = (((0,), (0,)), ((), ()))
NN = (((1,), (0,)), ((), ()))


def position():
    row, col = lax.axis_index("row"), lax.axis_index("col")
    return {
        "core": lax.rem(row, 2),
        "y": lax.rem(lax.div(row, 2), NY),
        "x": lax.div(row, 2 * NY) * 2 + lax.rem(col, 2),
        "z": lax.div(col, 2),
    }


def device(me, off):
    at = dict(me)
    for axis, k in off.items():
        at[axis] = lax.rem(me[axis] + (k + SIZES[axis]), SIZES[axis])
    row = lax.div(at["x"], 2) * (2 * NY) + at["y"] * 2 + at["core"]
    return (row, at["z"] * 2 + lax.rem(at["x"], 2))


def half(j):
    return 1 if 2 <= j % NY <= 5 else 0


def spot(j):
    return j % NY - 2 if half(j) else (0, 1, None, None, None, None, 2, 3)[j % NY]


def dot(a, b, dims):
    return lax.dot_general(a, b, dims, preferred_element_type=F32)


def kernel(
    nef_ref, bias_ref, ded_in, t_ref, w_ref, gap_in, pos_in, colgap_in,
    out_ref,
    ded_ref, gap_ref, pos_ref, colgap_ref,
    xg, yg, oh, pt, sim, dm, slope, slope_lo,
    dx, dx_core, dx_send, dx_far, dx_half, dx_near, dx_mid, dx_next,
    dy, x1_send, x1_recv, y_send, y_far, y_half, y_near, y_next, y_sum, x2_recv,
    st_x, st_z, st_y,
    local_sem, send_sem, recv_sem,
):
    me = position()
    ids = {(axis, k): device(me, {axis: k}) for axis, k in GROUP}
    barrier = pltpu.get_barrier_semaphore()
    for near in NEAR:
        pl.semaphore_signal(barrier, inc=1, device_id=ids[near], device_id_type=MESH)

    fetched = []
    for src, dst in (
        (gap_in, gap_ref),
        (pos_in, pos_ref),
        (colgap_in, colgap_ref),
        (w_ref, yg.at[pl.ds(0, YR), pl.ds(0, D)]),
        (t_ref, xg.at[pl.ds(0, XR), pl.ds(0, D)]),
        (ded_in, ded_ref),
    ):
        copy = pltpu.make_async_copy(src, dst, local_sem.at[len(fetched)])
        copy.start()
        fetched.append(copy)

    started = []

    def send(src, dst, axis, k):
        return send_to(src, dst, ids[axis, k % SIZES[axis]])

    def send_to(src, dst, there):
        i = len(started)
        copy = pltpu.make_async_remote_copy(
            src_ref=src,
            dst_ref=dst,
            send_sem=send_sem.at[i],
            recv_sem=recv_sem.at[i],
            device_id=there,
            device_id_type=MESH,
        )
        copy.start()
        started.append(copy)
        return copy

    for copy in fetched:
        copy.wait()
    lane = lax.broadcasted_iota(jnp.int32, (XR, 128), 1)

    def column(ref, n):
        diagonal = lax.broadcasted_iota(jnp.int32, (n, n), 0) == lax.broadcasted_iota(
            jnp.int32, (n, n), 1
        )
        row = jnp.broadcast_to(ref[...].astype(F32), (n, n))
        return jnp.sum(jnp.where(diagonal, row, 0.0), axis=1, keepdims=True)

    gap, pos = column(gap_ref, XR), column(pos_ref, XR)
    pos_high = jnp.floor(pos * (1.0 / 128.0))
    pos_low = pos - 128.0 * pos_high
    extra = jnp.where(
        lane == 0, gap, jnp.where(lane == 1, pos_high, jnp.where(lane == 2, pos_low, 0.0))
    )
    xg[0:XR, D:DE] = extra.astype(BF16)
    yg[0:YR, D:DE] = jnp.broadcast_to(column(colgap_ref, YR), (YR, 128)).astype(BF16)

    pl.semaphore_wait(barrier, len(NEAR))

    def xs(k):
        return xg.at[pl.ds((k % NZ) * XR, XR)]

    def xs_other(k):
        return xg.at[pl.ds(HALF + (k % NZ) * XR, XR)]

    def ys(i, j):
        return yg.at[pl.ds(half(j) * 256 + PLACE[i % NX] * 64 + spot(j) * YR, YR)]

    lo_cols, hi_cols = pl.ds(0, 512), pl.ds(512, DE - 512)
    xp, xm, core = {}, {}, {}

    def to_x(j):
        xp[j] = send(ys(0, j), ys(-1, j), "x", 1)
        xm[j] = send(ys(0, j), ys(1, j), "x", -1)

    def to_core(k):
        core[k] = send(xs(k), xs_other(k), "core", 1)

    x2 = send(ys(0, 0), ys(-2, 0), "x", 2)
    yp1 = send(ys(0, 0), ys(0, -1), "y", 1)
    ym1 = send(ys(0, 0), ys(0, 1), "y", -1)
    yp2 = send(ys(0, 0), ys(0, -2), "y", 2)
    ym2 = send(ys(0, 0), ys(0, 2), "y", -2)
    to_x(0)
    zp2 = send(xs(0), xs(-2), "z", 2)
    zm2 = send(xs(0), xs(2), "z", -2)
    zp1 = send(xs(0), xs(-1), "z", 1)
    zm1 = send(xs(0), xs(1), "z", -1)
    to_core(0)

    yp1.wait_recv()
    to_x(-1)
    ym1.wait_recv()
    to_x(1)
    x2.wait_recv()
    fp2 = send(ys(2, 0), ys(2, -2), "y", 2)
    fm2 = send(ys(2, 0), ys(2, 2), "y", -2)
    yp2.wait_recv()
    yp4 = send(ys(0, -2).at[:, lo_cols], ys(0, 4).at[:, lo_cols], "y", 2)
    yp3 = send(ys(0, -2), ys(0, -3), "y", 1)
    to_x(-2)
    ym2.wait_recv()
    ym4 = send(ys(0, 2).at[:, hi_cols], ys(0, 4).at[:, hi_cols], "y", -2)
    ym3 = send(ys(0, 2), ys(0, 3), "y", -1)
    fp1 = send(ys(2, 0), ys(2, -1), "y", 1)
    fm1 = send(ys(2, 0), ys(2, 1), "y", -1)
    to_x(2)
    zp2.wait_recv()
    zp4 = send(xs(-2).at[pl.ds(0, 16)], xs(4).at[pl.ds(0, 16)], "z", 2)
    zp3 = send(xs(-2), xs(-3), "z", 1)
    zm2.wait_recv()
    zm4 = send(xs(2).at[pl.ds(16, 16)], xs(4).at[pl.ds(16, 16)], "z", -2)
    zm3 = send(xs(2), xs(3), "z", -1)
    to_core(-2)
    to_core(2)
    fp2.wait_recv()
    fp4 = send(ys(2, -2).at[:, lo_cols], ys(2, 4).at[:, lo_cols], "y", 2)
    fp3 = send(ys(2, -2), ys(2, -3), "y", 1)
    fm2.wait_recv()
    fm4 = send(ys(2, 2).at[:, hi_cols], ys(2, 4).at[:, hi_cols], "y", -2)
    fm3 = send(ys(2, 2), ys(2, 3), "y", -1)
    yp3.wait_recv()
    to_x(-3)
    ym3.wait_recv()
    to_x(3)
    yp4.wait_recv()
    ym4.wait_recv()
    to_x(4)
    zp1.wait_recv()
    to_core(-1)
    zm1.wait_recv()
    to_core(1)
    zp3.wait_recv()
    to_core(-3)
    zm3.wait_recv()
    to_core(3)
    zp4.wait_recv()
    zm4.wait_recv()
    to_core(4)
    for copy in core.values():
        copy.wait_recv()
    lane = lax.broadcasted_iota(jnp.int32, (NR, 128), 1)
    lane16 = (lane % 16).astype(F32)
    gap = xg[:, D:DE].astype(F32)[:, 0:1]
    oh[...] = jnp.where((lane16 == gap) & (lane < 48), 1.0, 0.0).astype(BF16)

    def tables(lo, hi):
        lane = lax.broadcasted_iota(jnp.int32, (hi - lo, 128), 1)
        apart = jnp.abs((lane % 16).astype(F32) - yg[lo:hi, D:DE].astype(F32))
        table = jnp.full((hi - lo, 128), ded_ref[7], F32)
        for k in range(7):
            table = jnp.where(apart == float(k), ded_ref[k], table)
        table = table - jnp.broadcast_to(bias_ref[...], (hi - lo, 128))
        first = table.astype(BF16)
        rest = table - first.astype(F32)
        second = rest.astype(BF16).astype(F32)
        third = (rest - second).astype(BF16).astype(F32)
        terms = jnp.where(lane < 32, second, jnp.where(lane < 48, third, 0.0))
        pt[lo:hi, :] = jnp.where(lane < 16, first.astype(F32), terms).astype(BF16)

    def group(lo, hi, step, sums):
        n = hi - lo
        tables(lo, hi)
        sim[:, lo:hi] = dot(xg[:, 0:D], yg[lo:hi, 0:D], NT)
        dm[:, lo:hi] = dot(oh[...], pt[lo:hi, :], NT)
        scale = jnp.exp(jnp.broadcast_to(nef_ref[...], (step, n)))
        at_lane = lax.broadcasted_iota(jnp.int32, (1, n), 1) + lo
        place = at_lane % 256 // 64
        from_x = jnp.where(place == 2, 3, jnp.where(place == 3, 2, place))
        at_spot = at_lane % 64 // YR
        from_y = jnp.where(at_lane >= 256, at_spot + 2, jnp.where(at_spot < 2, at_spot, at_spot + 4))
        win_y = (from_y + me["y"]) % NY
        win_x = (from_x + me["x"]) % NX
        win_row = (win_x // 2) * (2 * NY) + win_y * 2 + me["core"]
        ordinal = (me["z"] * 2 + win_x % 2) * 512 + win_row * YR + at_lane % YR
        ordinal = ordinal.astype(F32)

        def slopes(b, sums):
            at = pl.ds(b * step if step == NR else pl.multiple_of(b * step, step), step)
            loss_sum, temp_sum = sums
            s = scale * sim[at, lo:hi]
            logit = s - dm[at, lo:hi]
            mine = xg[at, D:DE].astype(F32)
            match = (mine[:, 1:2] * 128.0 + mine[:, 2:3]) == ordinal
            z = jnp.where(match, -logit, logit)
            e = jnp.exp(-jnp.abs(z))
            r = 1.0 / (1.0 + e)
            sig = jnp.where(z >= 0.0, r, e * r)
            grad = jnp.where(match, -sig, sig)
            loss = jnp.maximum(z, 0.0) + jnp.log1p(e)
            temp = grad * s
            high = grad.astype(BF16)
            slope[at, lo:hi] = high
            slope_lo[at, lo:hi] = (grad - high.astype(F32)).astype(BF16)
            for i in range(0, step, 16):
                for j in range(0, n, 128):
                    loss_sum = loss_sum + loss[i : i + 16, j : j + 128]
                    temp_sum = temp_sum + temp[i : i + 16, j : j + 128]
            return loss_sum, temp_sum

        if step == NR:
            loss_sum, temp_sum = slopes(0, sums)
        else:
            loss_sum, temp_sum = lax.fori_loop(0, NR // step, slopes, sums)

        by_gap = dot(slope[:, lo:hi], oh[...], TN) + dot(slope_lo[:, lo:hi], oh[...], TN)
        lane = lax.broadcasted_iota(jnp.int32, (n, 128), 1)
        apart = jnp.abs((lane % 16).astype(F32) - yg[lo:hi, D:DE].astype(F32))
        apart = jnp.where(lane < 16, jnp.minimum(apart, 7.0), 8.0)
        buckets = [
            jnp.sum(jnp.where(apart == float(k), by_gap, 0.0), axis=0, keepdims=True)
            for k in range(8)
        ]
        return loss_sum, temp_sum, buckets

    zero = jnp.zeros((16, 128), F32)
    fp1.wait_recv()
    fm1.wait_recv()
    for j in (0, -1, 1, -2):
        xp[j].wait_recv()
        xm[j].wait_recv()
    loss_sum, temp_sum, first = group(0, 256, 128, (zero, zero))
    for copy in (fp3, fm3, fp4, fm4):
        copy.wait_recv()
    for j in (2, -3, 3, 4):
        xp[j].wait_recv()
        xm[j].wait_recv()
    loss_sum, temp_sum, second = group(256, 512, NR, (loss_sum, temp_sum))

    row_s = lax.broadcasted_iota(jnp.int32, (16, 128), 0)
    stats = jnp.where(row_s == 8, jnp.sum(loss_sum, axis=0, keepdims=True), 0.0)
    stats = jnp.where(row_s == 9, jnp.sum(temp_sum, axis=0, keepdims=True), stats)
    for k in range(8):
        stats = jnp.where(row_s == k, -(first[k] + second[k]), stats)

    def share(value, slots, a, b):
        here = me[a] * SIZES[b] + me[b] if b else me[a]
        slots[here] = value
        return [
            send_to(slots.at[here], slots.at[here], device(me, {a: i, b: j} if b else {a: i}))
            for j in range(SIZES[b] if b else 1)
            for i in range(SIZES[a])
            if i + j > 0
        ]

    def summed(copies, slots):
        for copy in copies:
            copy.wait_recv()
        value = slots[0]
        for k in range(1, slots.shape[0]):
            value = value + slots[k]
        return value

    stat_x = share(stats, st_x, "x", "core")

    def win_grad(lo, hi):
        dy[lo:hi, :] = dot(slope[:, lo:hi], xg[:, 0:D], TN)

    def time_grad(lo):
        dx[lo : lo + HALF, :] = dot(slope[lo : lo + HALF, :], yg[:, 0:D], NN)

    class AlongY:
        def __init__(self, tag, part):
            self.out, self.part = y_send.at[tag], part
            self.far, self.mid = y_far.at[tag], y_half.at[tag]
            self.near, self.next = y_near.at[tag], y_next.at[tag]

        def fill(self, slot, value):
            self.out[slot] = value.astype(BF16)
            return self.out.at[slot]

        def first(self):
            across = self.fill(2, self.part(4))
            self.c4 = (
                send(across.at[:, pl.ds(0, 512)], self.mid.at[0], "y", 2),
                send(across.at[:, pl.ds(512, 512)], self.mid.at[1], "y", -2),
            )
            self.c3 = (
                send(self.fill(0, self.part(3)), self.far.at[0], "y", 1),
                send(self.fill(1, self.part(5)), self.far.at[1], "y", -1),
            )

        def nearest(self):
            self.c1 = (
                send(self.fill(3, self.part(1)), self.near.at[0], "y", 1),
                send(self.fill(4, self.part(7)), self.near.at[1], "y", -1),
            )

        def second(self):
            self.c2 = []
            for side, j in ((0, 2), (1, 6)):
                self.c3[side].wait_recv()
                self.c4[side].wait_recv()
                value = self.part(j) + self.far[side].astype(F32)
                low, high = value[:, 0:512], value[:, 512:1024]
                passing = self.mid[side].astype(F32)
                if side == 0:
                    low = low + passing
                else:
                    high = high + passing
                self.out[5 + side, :, 0:512] = low.astype(BF16)
                self.out[5 + side, :, 512:1024] = high.astype(BF16)
                self.c2.append(
                    send(self.out.at[5 + side], self.next.at[side], "y", 2 if side == 0 else -2)
                )

        def total(self):
            for copy in (*self.c1, *self.c2):
                copy.wait_recv()
            value = self.part(0)
            for arrived in (self.near, self.next):
                value = value + arrived[0].astype(F32) + arrived[1].astype(F32)
            return value

    def start(j, block):
        return half(j) * 256 + block * 64 + spot(j) * YR

    def two_away(j):
        return dy[start(j, 3) : start(j, 3) + YR, :]

    def own_column(j):
        q = spot(j) * YR
        value = dy[start(j, 0) : start(j, 0) + YR, :]
        for side in (0, 1):
            value = value + x1_recv[side, half(j), q : q + YR, :].astype(F32)
        return value

    x1 = {}

    def x1_to(h):
        for side in (0, 1):
            lo = h * 256 + 64 + side * 64
            x1_send[side, h] = dy[lo : lo + 64, :].astype(BF16)
        for p, n in ((1, 3), (0, 1)) if h else ((0, 4),):
            at = pl.ds(p * YR, n * YR)
            for side, k in ((0, 1), (1, -1)):
                x1[side, h, p] = send(x1_send.at[side, h, at], x1_recv.at[side, h, at], "x", k)

    passing, column = AlongY(0, two_away), AlongY(1, own_column)
    win_grad(256, 512)
    passing.first()
    x1_to(1)

    time_grad(HALF)
    swaps = []
    for lo, n in ((3, 3), (6, 2), (0, 3)):
        at, to = pl.ds(HALF + lo * XR, n * XR), pl.ds(lo * XR, n * XR)
        swaps.append(send(dx.at[at], dx_core.at[to], "core", 1))
    win_grad(0, 256)
    x1_to(0)
    passing.nearest()
    time_grad(0)

    def own(k):
        at = pl.ds((k % NZ) * XR, XR)
        return dx[at, :] + dx_core[at, :]

    swaps[0].wait_recv()
    dx_send[2] = own(4).astype(BF16)
    z4p = send(dx_send.at[2, pl.ds(0, 16)], dx_half.at[0], "z", 2)
    z4m = send(dx_send.at[2, pl.ds(16, 16)], dx_half.at[1], "z", -2)
    dx_send[0] = own(3).astype(BF16)
    z3p = send(dx_send.at[0], dx_far.at[0], "z", 1)
    dx_send[1] = own(-3).astype(BF16)
    z3m = send(dx_send.at[1], dx_far.at[1], "z", -1)
    stat_y = share(summed(stat_x, st_x), st_y, "y", None)
    swaps[1].wait_recv()
    swaps[2].wait_recv()
    dx_send[3] = own(1).astype(BF16)
    z1p = send(dx_send.at[3], dx_near.at[0], "z", 1)
    dx_send[4] = own(-1).astype(BF16)
    z1m = send(dx_send.at[4], dx_near.at[1], "z", -1)
    dx_mid[0] = own(2)
    dx_mid[1] = own(-2)
    passing.second()
    x1[0, 1, 1].wait_recv()
    x1[1, 1, 1].wait_recv()
    column.first()

    z3p.wait_recv()
    z4p.wait_recv()
    part = dx_mid[0] + dx_far[0].astype(F32)
    dx_send[5, 0:16] = (part[0:16] + dx_half[0].astype(F32)).astype(BF16)
    dx_send[5, 16:32] = part[16:32].astype(BF16)
    z2p = send(dx_send.at[5], dx_next.at[0], "z", 2)
    z3m.wait_recv()
    z4m.wait_recv()
    part = dx_mid[1] + dx_far[1].astype(F32)
    dx_send[6, 0:16] = part[0:16].astype(BF16)
    dx_send[6, 16:32] = (part[16:32] + dx_half[1].astype(F32)).astype(BF16)
    z2m = send(dx_send.at[6], dx_next.at[1], "z", -2)

    for side in (0, 1):
        x1[side, 1, 0].wait_recv()
        x1[side, 0, 0].wait_recv()
    column.nearest()
    y_sum[...] = passing.total().astype(BF16)
    x2_done = send(y_sum, x2_recv, "x", 2)
    stat_z = share(summed(stat_y, st_y), st_z, "z", None)
    column.second()

    temperature = jnp.exp(jnp.broadcast_to(nef_ref[...], (XR, D)))
    for copy in (z1p, z1m, z2p, z2m):
        copy.wait_recv()
    full = own(0) + dx_near[0].astype(F32) + dx_near[1].astype(F32)
    full = full + dx_next[0].astype(F32) + dx_next[1].astype(F32)
    out_ref[0:XR, :] = temperature * full

    stats = jnp.sum(summed(stat_z, st_z), axis=1, keepdims=True) * (1.0 / PAIRS)
    lane_s = lax.broadcasted_iota(jnp.int32, (8, 128), 1)
    diagonal = lax.broadcasted_iota(jnp.int32, (8, 128), 0) == lane_s
    buckets = jnp.sum(jnp.where(diagonal, stats[0:8], 0.0), axis=0, keepdims=True)
    row_s = lax.broadcasted_iota(jnp.int32, (8, 128), 0)
    out = jnp.where(row_s == 0, buckets, 0.0)
    out = jnp.where(row_s == 1, stats[8:9], out)
    out = jnp.where(row_s == 2, stats[9:10], out)
    out = jnp.where(row_s == 3, -jnp.sum(stats[0:8], axis=0, keepdims=True), out)
    out_ref[XR + YR : XR + YR + 8, 0:128] = out

    mine = column.total()
    x2_done.wait_recv()
    mine = mine + x2_recv[...].astype(F32)
    out_ref[XR : XR + YR, :] = temperature[0:YR] * mine

    for copy in started:
        copy.wait_send()


COPIES = 192


def finish(packed, loss, gt, gw, bias, temp, penalty):
    gt[...] = packed[0:XR, :]
    gw[...] = packed[XR : XR + YR, :].reshape(YR, 1, D)
    penalty[...] = packed[XR + YR, 0:8]
    loss[...] = packed[XR + YR + 1, 0:1]
    temp[...] = packed[XR + YR + 2, 0:1]
    bias[...] = packed[XR + YR + 3, 0:1]


def local(timelines, windows, row_gap, col_gap, positive, nef, bias, deduction):
    vmem = pl.BlockSpec(memory_space=pltpu.VMEM)
    anywhere = pl.BlockSpec(memory_space=pltpu.HBM)
    shape = jax.ShapeDtypeStruct
    packed = pl.pallas_call(
        kernel,
        out_shape=shape((XR + YR + 8, D), F32),
        in_specs=[vmem] * 2 + [anywhere] * 6,
        out_specs=vmem,
        scratch_shapes=[
            pltpu.SMEM((8,), F32),
            pltpu.VMEM((1, XR), jnp.int32),
            pltpu.VMEM((1, XR), jnp.int32),
            pltpu.VMEM((1, YR), jnp.int32),
            pltpu.VMEM((NR, DE), BF16),
            pltpu.VMEM((NW, DE), BF16),
            pltpu.VMEM((NR, 128), BF16),
            pltpu.VMEM((NW, 128), BF16),
            pltpu.VMEM((NR, NW), F32),
            pltpu.VMEM((NR, NW), F32),
            pltpu.VMEM((NR, NW), BF16),
            pltpu.VMEM((NR, NW), BF16),
            pltpu.VMEM((NR, D), F32),
            pltpu.VMEM((HALF, D), F32),
            pltpu.VMEM((7, XR, D), BF16),
            pltpu.VMEM((2, XR, D), BF16),
            pltpu.VMEM((2, 16, D), BF16),
            pltpu.VMEM((2, XR, D), BF16),
            pltpu.VMEM((2, XR, D), F32),
            pltpu.VMEM((2, XR, D), BF16),
            pltpu.VMEM((NW, D), F32),
            pltpu.VMEM((2, 2, 64, D), BF16),
            pltpu.VMEM((2, 2, 64, D), BF16),
            pltpu.VMEM((2, 7, YR, D), BF16),
            pltpu.VMEM((2, 2, YR, D), BF16),
            pltpu.VMEM((2, 2, YR, 512), BF16),
            pltpu.VMEM((2, 2, YR, D), BF16),
            pltpu.VMEM((2, 2, YR, D), BF16),
            pltpu.VMEM((YR, D), BF16),
            pltpu.VMEM((YR, D), BF16),
            pltpu.VMEM((NX * 2, 16, 128), F32),
            pltpu.VMEM((NZ, 16, 128), F32),
            pltpu.VMEM((NY, 16, 128), F32),
            pltpu.SemaphoreType.DMA((6,)),
            pltpu.SemaphoreType.DMA((COPIES,)),
            pltpu.SemaphoreType.DMA((COPIES,)),
        ],
        compiler_params=pltpu.CompilerParams(
            collective_id=0, has_side_effects=True, vmem_limit_bytes=56 << 20
        ),
        name="loss_and_gradients",
    )(
        nef.reshape(1, 1), bias.reshape(1, 1), deduction, timelines, windows.reshape(YR, D),
        row_gap.reshape(1, XR), positive.reshape(1, XR), col_gap.reshape(1, YR),
    )
    return pl.pallas_call(
        finish,
        out_shape=(
            shape((1,), F32), shape((XR, D), F32), shape((YR, 1, D), F32),
            shape((1,), F32), shape((1,), F32), shape((8,), F32),
        ),
        in_specs=[vmem],
        out_specs=(vmem,) * 6,
        name="finish",
    )(packed)


def solution(mesh):
    return jax.shard_map(
        local,
        mesh=mesh,
        in_specs=(
            P(("row", "col"), None),
            P("row", "col", None),
            P(("row", "col")),
            P("row", "col"),
            P(("row", "col")),
            P(),
            P(),
            P(),
        ),
        out_specs=(P(), P(("row", "col"), None), P("row", "col", None), P(), P(), P()),
        check_vma=False,
    )
```

```python
import jax
import jax.numpy as jnp
from jax import lax
from jax.experimental import pallas as pl
from jax.experimental.pallas import tpu as pltpu
from jax.sharding import PartitionSpec as P

MESH = pl.DeviceIdType.MESH
F32 = jnp.float32
BF16 = jnp.bfloat16

D = 1024
DE = D + 128
XR = 32
YR = 16
NZ, NY, NX = 8, 8, 4
NR = XR * NZ * 2
NW = YR * NY * NX
HALF = NR // 2
PAIRS = 134217728
SIZES = {"core": 2, "x": NX, "y": NY, "z": NZ}
GROUP = [(axis, k) for axis in SIZES for k in range(1, SIZES[axis])]
NEAR = [(axis, k) for axis, k in GROUP if min(k, SIZES[axis] - k) <= 2]
PLACE = (0, 1, 3, 2)
NT = (((1,), (1,)), ((), ()))
TN = (((0,), (0,)), ((), ()))
NN = (((1,), (0,)), ((), ()))


def position():
    row, col = lax.axis_index("row"), lax.axis_index("col")
    return {
        "core": lax.rem(row, 2),
        "y": lax.rem(lax.div(row, 2), NY),
        "x": lax.div(row, 2 * NY) * 2 + lax.rem(col, 2),
        "z": lax.div(col, 2),
    }


def device(me, off):
    at = dict(me)
    for axis, k in off.items():
        at[axis] = lax.rem(me[axis] + (k + SIZES[axis]), SIZES[axis])
    row = lax.div(at["x"], 2) * (2 * NY) + at["y"] * 2 + at["core"]
    return (row, at["z"] * 2 + lax.rem(at["x"], 2))


def half(j):
    return 1 if 2 <= j % NY <= 5 else 0


def spot(j):
    return j % NY - 2 if half(j) else (0, 1, None, None, None, None, 2, 3)[j % NY]


def dot(a, b, dims):
    return lax.dot_general(a, b, dims, preferred_element_type=F32)


def kernel(
    nef_ref, bias_ref, ded_in, t_ref, w_ref, gap_in, pos_in, colgap_in,
    out_ref,
    ded_ref, gap_ref, pos_ref, colgap_ref,
    xg, yg, oh, pt, sim, dm, slope, slope_lo,
    dx, dx_core, dx_send, dx_far, dx_half, dx_near, dx_mid, dx_next,
    dy, x1_send, x1_recv, y_send, y_far, y_half, y_near, y_next, y_sum, x2_recv,
    st_x, st_z, st_y,
    local_sem, send_sem, recv_sem,
):
    me = position()
    ids = {(axis, k): device(me, {axis: k}) for axis, k in GROUP}
    barrier = pltpu.get_barrier_semaphore()
    for near in NEAR:
        pl.semaphore_signal(barrier, inc=1, device_id=ids[near], device_id_type=MESH)

    fetched = []
    for src, dst in (
        (gap_in, gap_ref),
        (pos_in, pos_ref),
        (colgap_in, colgap_ref),
        (w_ref, yg.at[pl.ds(0, YR), pl.ds(0, D)]),
        (t_ref, xg.at[pl.ds(0, XR), pl.ds(0, D)]),
        (ded_in, ded_ref),
    ):
        copy = pltpu.make_async_copy(src, dst, local_sem.at[len(fetched)])
        copy.start()
        fetched.append(copy)

    started = []

    def send(src, dst, axis, k):
        return send_to(src, dst, ids[axis, k % SIZES[axis]])

    def send_to(src, dst, there):
        i = len(started)
        copy = pltpu.make_async_remote_copy(
            src_ref=src,
            dst_ref=dst,
            send_sem=send_sem.at[i],
            recv_sem=recv_sem.at[i],
            device_id=there,
            device_id_type=MESH,
        )
        copy.start()
        started.append(copy)
        return copy

    for copy in fetched:
        copy.wait()
    lane = lax.broadcasted_iota(jnp.int32, (XR, 128), 1)

    def column(ref, n):
        diagonal = lax.broadcasted_iota(jnp.int32, (n, n), 0) == lax.broadcasted_iota(
            jnp.int32, (n, n), 1
        )
        row = jnp.broadcast_to(ref[...].astype(F32), (n, n))
        return jnp.sum(jnp.where(diagonal, row, 0.0), axis=1, keepdims=True)

    gap, pos = column(gap_ref, XR), column(pos_ref, XR)
    pos_high = jnp.floor(pos * (1.0 / 128.0))
    pos_low = pos - 128.0 * pos_high
    extra = jnp.where(
        lane == 0, gap, jnp.where(lane == 1, pos_high, jnp.where(lane == 2, pos_low, 0.0))
    )
    xg[0:XR, D:DE] = extra.astype(BF16)
    yg[0:YR, D:DE] = jnp.broadcast_to(column(colgap_ref, YR), (YR, 128)).astype(BF16)

    pl.semaphore_wait(barrier, len(NEAR))

    def xs(k):
        return xg.at[pl.ds((k % NZ) * XR, XR)]

    def xs_other(k):
        return xg.at[pl.ds(HALF + (k % NZ) * XR, XR)]

    def ys(i, j):
        return yg.at[pl.ds(half(j) * 256 + PLACE[i % NX] * 64 + spot(j) * YR, YR)]

    lo_cols, hi_cols = pl.ds(0, 512), pl.ds(512, DE - 512)
    xp, xm, core = {}, {}, {}

    def to_x(j):
        xp[j] = send(ys(0, j), ys(-1, j), "x", 1)
        xm[j] = send(ys(0, j), ys(1, j), "x", -1)

    def to_core(k):
        core[k] = send(xs(k), xs_other(k), "core", 1)

    x2 = send(ys(0, 0), ys(-2, 0), "x", 2)
    yp1 = send(ys(0, 0), ys(0, -1), "y", 1)
    ym1 = send(ys(0, 0), ys(0, 1), "y", -1)
    yp2 = send(ys(0, 0), ys(0, -2), "y", 2)
    ym2 = send(ys(0, 0), ys(0, 2), "y", -2)
    to_x(0)
    zp2 = send(xs(0), xs(-2), "z", 2)
    zm2 = send(xs(0), xs(2), "z", -2)
    zp1 = send(xs(0), xs(-1), "z", 1)
    zm1 = send(xs(0), xs(1), "z", -1)
    to_core(0)

    yp1.wait_recv()
    to_x(-1)
    ym1.wait_recv()
    to_x(1)
    x2.wait_recv()
    fp2 = send(ys(2, 0), ys(2, -2), "y", 2)
    fm2 = send(ys(2, 0), ys(2, 2), "y", -2)
    yp2.wait_recv()
    yp4 = send(ys(0, -2).at[:, lo_cols], ys(0, 4).at[:, lo_cols], "y", 2)
    yp3 = send(ys(0, -2), ys(0, -3), "y", 1)
    to_x(-2)
    ym2.wait_recv()
    ym4 = send(ys(0, 2).at[:, hi_cols], ys(0, 4).at[:, hi_cols], "y", -2)
    ym3 = send(ys(0, 2), ys(0, 3), "y", -1)
    fp1 = send(ys(2, 0), ys(2, -1), "y", 1)
    fm1 = send(ys(2, 0), ys(2, 1), "y", -1)
    to_x(2)
    zp2.wait_recv()
    zp4 = send(xs(-2).at[pl.ds(0, 16)], xs(4).at[pl.ds(0, 16)], "z", 2)
    zp3 = send(xs(-2), xs(-3), "z", 1)
    zm2.wait_recv()
    zm4 = send(xs(2).at[pl.ds(16, 16)], xs(4).at[pl.ds(16, 16)], "z", -2)
    zm3 = send(xs(2), xs(3), "z", -1)
    to_core(-2)
    to_core(2)
    fp2.wait_recv()
    fp4 = send(ys(2, -2).at[:, lo_cols], ys(2, 4).at[:, lo_cols], "y", 2)
    fp3 = send(ys(2, -2), ys(2, -3), "y", 1)
    fm2.wait_recv()
    fm4 = send(ys(2, 2).at[:, hi_cols], ys(2, 4).at[:, hi_cols], "y", -2)
    fm3 = send(ys(2, 2), ys(2, 3), "y", -1)
    yp3.wait_recv()
    to_x(-3)
    ym3.wait_recv()
    to_x(3)
    yp4.wait_recv()
    ym4.wait_recv()
    to_x(4)
    zp1.wait_recv()
    to_core(-1)
    zm1.wait_recv()
    to_core(1)
    zp3.wait_recv()
    to_core(-3)
    zm3.wait_recv()
    to_core(3)
    zp4.wait_recv()
    zm4.wait_recv()
    to_core(4)
    for copy in core.values():
        copy.wait_recv()
    lane = lax.broadcasted_iota(jnp.int32, (NR, 128), 1)
    lane16 = (lane % 16).astype(F32)
    gap = xg[:, D:DE].astype(F32)[:, 0:1]
    oh[...] = jnp.where((lane16 == gap) & (lane < 48), 1.0, 0.0).astype(BF16)

    def tables(lo, hi):
        lane = lax.broadcasted_iota(jnp.int32, (hi - lo, 128), 1)
        apart = jnp.abs((lane % 16).astype(F32) - yg[lo:hi, D:DE].astype(F32))
        table = jnp.full((hi - lo, 128), ded_ref[7], F32)
        for k in range(7):
            table = jnp.where(apart == float(k), ded_ref[k], table)
        table = table - jnp.broadcast_to(bias_ref[...], (hi - lo, 128))
        first = table.astype(BF16)
        rest = table - first.astype(F32)
        second = rest.astype(BF16).astype(F32)
        third = (rest - second).astype(BF16).astype(F32)
        terms = jnp.where(lane < 32, second, jnp.where(lane < 48, third, 0.0))
        pt[lo:hi, :] = jnp.where(lane < 16, first.astype(F32), terms).astype(BF16)

    def group(lo, hi, step, sums):
        n = hi - lo
        tables(lo, hi)
        sim[:, lo:hi] = dot(xg[:, 0:D], yg[lo:hi, 0:D], NT)
        dm[:, lo:hi] = dot(oh[...], pt[lo:hi, :], NT)
        scale = jnp.exp(jnp.broadcast_to(nef_ref[...], (step, n)))
        at_lane = lax.broadcasted_iota(jnp.int32, (1, n), 1) + lo
        place = at_lane % 256 // 64
        from_x = jnp.where(place == 2, 3, jnp.where(place == 3, 2, place))
        at_spot = at_lane % 64 // YR
        from_y = jnp.where(at_lane >= 256, at_spot + 2, jnp.where(at_spot < 2, at_spot, at_spot + 4))
        win_y = (from_y + me["y"]) % NY
        win_x = (from_x + me["x"]) % NX
        win_row = (win_x // 2) * (2 * NY) + win_y * 2 + me["core"]
        ordinal = (me["z"] * 2 + win_x % 2) * 512 + win_row * YR + at_lane % YR
        ordinal = ordinal.astype(F32)

        def slopes(b, sums):
            at = pl.ds(b * step if step == NR else pl.multiple_of(b * step, step), step)
            loss_sum, temp_sum = sums
            s = scale * sim[at, lo:hi]
            logit = s - dm[at, lo:hi]
            mine = xg[at, D:DE].astype(F32)
            match = (mine[:, 1:2] * 128.0 + mine[:, 2:3]) == ordinal
            z = jnp.where(match, -logit, logit)
            e = jnp.exp(-jnp.abs(z))
            r = 1.0 / (1.0 + e)
            sig = jnp.where(z >= 0.0, r, e * r)
            grad = jnp.where(match, -sig, sig)
            loss = jnp.maximum(z, 0.0) + jnp.log1p(e)
            temp = grad * s
            high = grad.astype(BF16)
            slope[at, lo:hi] = high
            slope_lo[at, lo:hi] = (grad - high.astype(F32)).astype(BF16)
            for i in range(0, step, 16):
                for j in range(0, n, 128):
                    loss_sum = loss_sum + loss[i : i + 16, j : j + 128]
                    temp_sum = temp_sum + temp[i : i + 16, j : j + 128]
            return loss_sum, temp_sum

        if step == NR:
            loss_sum, temp_sum = slopes(0, sums)
        else:
            loss_sum, temp_sum = lax.fori_loop(0, NR // step, slopes, sums)

        by_gap = dot(slope[:, lo:hi], oh[...], TN) + dot(slope_lo[:, lo:hi], oh[...], TN)
        lane = lax.broadcasted_iota(jnp.int32, (n, 128), 1)
        apart = jnp.abs((lane % 16).astype(F32) - yg[lo:hi, D:DE].astype(F32))
        apart = jnp.where(lane < 16, jnp.minimum(apart, 7.0), 8.0)
        buckets = [
            jnp.sum(jnp.where(apart == float(k), by_gap, 0.0), axis=0, keepdims=True)
            for k in range(8)
        ]
        return loss_sum, temp_sum, buckets

    zero = jnp.zeros((16, 128), F32)
    fp1.wait_recv()
    fm1.wait_recv()
    for j in (0, -1, 1, -2):
        xp[j].wait_recv()
        xm[j].wait_recv()
    loss_sum, temp_sum, first = group(0, 256, 128, (zero, zero))
    for copy in (fp3, fm3, fp4, fm4):
        copy.wait_recv()
    for j in (2, -3, 3, 4):
        xp[j].wait_recv()
        xm[j].wait_recv()
    loss_sum, temp_sum, second = group(256, 512, NR, (loss_sum, temp_sum))

    row_s = lax.broadcasted_iota(jnp.int32, (16, 128), 0)
    stats = jnp.where(row_s == 8, jnp.sum(loss_sum, axis=0, keepdims=True), 0.0)
    stats = jnp.where(row_s == 9, jnp.sum(temp_sum, axis=0, keepdims=True), stats)
    for k in range(8):
        stats = jnp.where(row_s == k, -(first[k] + second[k]), stats)

    def share(value, slots, a, b):
        here = me[a] * SIZES[b] + me[b] if b else me[a]
        slots[here] = value
        return [
            send_to(slots.at[here], slots.at[here], device(me, {a: i, b: j} if b else {a: i}))
            for j in range(SIZES[b] if b else 1)
            for i in range(SIZES[a])
            if i + j > 0
        ]

    def summed(copies, slots):
        for copy in copies:
            copy.wait_recv()
        value = slots[0]
        for k in range(1, slots.shape[0]):
            value = value + slots[k]
        return value

    stat_x = share(stats, st_x, "x", "core")

    def win_grad(lo, hi):
        dy[lo:hi, :] = dot(slope[:, lo:hi], xg[:, 0:D], TN)

    def time_grad(lo):
        dx[lo : lo + HALF, :] = dot(slope[lo : lo + HALF, :], yg[:, 0:D], NN)

    class AlongY:
        def __init__(self, tag, part):
            self.out, self.part = y_send.at[tag], part
            self.far, self.mid = y_far.at[tag], y_half.at[tag]
            self.near, self.next = y_near.at[tag], y_next.at[tag]

        def fill(self, slot, value):
            self.out[slot] = value.astype(BF16)
            return self.out.at[slot]

        def first(self):
            across = self.fill(2, self.part(4))
            self.c4 = (
                send(across.at[:, pl.ds(0, 512)], self.mid.at[0], "y", 2),
                send(across.at[:, pl.ds(512, 512)], self.mid.at[1], "y", -2),
            )
            self.c3 = (
                send(self.fill(0, self.part(3)), self.far.at[0], "y", 1),
                send(self.fill(1, self.part(5)), self.far.at[1], "y", -1),
            )

        def nearest(self):
            self.c1 = (
                send(self.fill(3, self.part(1)), self.near.at[0], "y", 1),
                send(self.fill(4, self.part(7)), self.near.at[1], "y", -1),
            )

        def second(self):
            self.c2 = []
            for side, j in ((0, 2), (1, 6)):
                self.c3[side].wait_recv()
                self.c4[side].wait_recv()
                value = self.part(j) + self.far[side].astype(F32)
                low, high = value[:, 0:512], value[:, 512:1024]
                passing = self.mid[side].astype(F32)
                if side == 0:
                    low = low + passing
                else:
                    high = high + passing
                self.out[5 + side, :, 0:512] = low.astype(BF16)
                self.out[5 + side, :, 512:1024] = high.astype(BF16)
                self.c2.append(
                    send(self.out.at[5 + side], self.next.at[side], "y", 2 if side == 0 else -2)
                )

        def total(self):
            for copy in (*self.c1, *self.c2):
                copy.wait_recv()
            value = self.part(0)
            for arrived in (self.near, self.next):
                value = value + arrived[0].astype(F32) + arrived[1].astype(F32)
            return value

    def start(j, block):
        return half(j) * 256 + block * 64 + spot(j) * YR

    def two_away(j):
        return dy[start(j, 3) : start(j, 3) + YR, :]

    def own_column(j):
        q = spot(j) * YR
        value = dy[start(j, 0) : start(j, 0) + YR, :]
        for side in (0, 1):
            value = value + x1_recv[side, half(j), q : q + YR, :].astype(F32)
        return value

    x1 = {}

    def x1_to(h):
        for side in (0, 1):
            lo = h * 256 + 64 + side * 64
            x1_send[side, h] = dy[lo : lo + 64, :].astype(BF16)
        for p, n in ((1, 3), (0, 1)) if h else ((0, 4),):
            at = pl.ds(p * YR, n * YR)
            for side, k in ((0, 1), (1, -1)):
                x1[side, h, p] = send(x1_send.at[side, h, at], x1_recv.at[side, h, at], "x", k)

    passing, column = AlongY(0, two_away), AlongY(1, own_column)
    win_grad(256, 512)
    passing.first()
    x1_to(1)

    time_grad(HALF)
    swaps = []
    for lo, n in ((3, 3), (6, 2), (0, 3)):
        at, to = pl.ds(HALF + lo * XR, n * XR), pl.ds(lo * XR, n * XR)
        swaps.append(send(dx.at[at], dx_core.at[to], "core", 1))
    win_grad(0, 256)
    x1_to(0)
    passing.nearest()
    time_grad(0)

    def own(k):
        at = pl.ds((k % NZ) * XR, XR)
        return dx[at, :] + dx_core[at, :]

    swaps[0].wait_recv()
    dx_send[2] = own(4).astype(BF16)
    z4p = send(dx_send.at[2, pl.ds(0, 16)], dx_half.at[0], "z", 2)
    z4m = send(dx_send.at[2, pl.ds(16, 16)], dx_half.at[1], "z", -2)
    dx_send[0] = own(3).astype(BF16)
    z3p = send(dx_send.at[0], dx_far.at[0], "z", 1)
    dx_send[1] = own(-3).astype(BF16)
    z3m = send(dx_send.at[1], dx_far.at[1], "z", -1)
    stat_y = share(summed(stat_x, st_x), st_y, "y", None)
    swaps[1].wait_recv()
    swaps[2].wait_recv()
    dx_send[3] = own(1).astype(BF16)
    z1p = send(dx_send.at[3], dx_near.at[0], "z", 1)
    dx_send[4] = own(-1).astype(BF16)
    z1m = send(dx_send.at[4], dx_near.at[1], "z", -1)
    dx_mid[0] = own(2)
    dx_mid[1] = own(-2)
    passing.second()
    x1[0, 1, 1].wait_recv()
    x1[1, 1, 1].wait_recv()
    column.first()
    early = len(started)

    z3p.wait_recv()
    z4p.wait_recv()
    part = dx_mid[0] + dx_far[0].astype(F32)
    dx_send[5, 0:16] = (part[0:16] + dx_half[0].astype(F32)).astype(BF16)
    dx_send[5, 16:32] = part[16:32].astype(BF16)
    z2p = send(dx_send.at[5], dx_next.at[0], "z", 2)
    z3m.wait_recv()
    z4m.wait_recv()
    part = dx_mid[1] + dx_far[1].astype(F32)
    dx_send[6, 0:16] = part[0:16].astype(BF16)
    dx_send[6, 16:32] = (part[16:32] + dx_half[1].astype(F32)).astype(BF16)
    z2m = send(dx_send.at[6], dx_next.at[1], "z", -2)

    for side in (0, 1):
        x1[side, 1, 0].wait_recv()
        x1[side, 0, 0].wait_recv()
    column.nearest()
    y_sum[...] = passing.total().astype(BF16)
    x2_done = send(y_sum, x2_recv, "x", 2)
    stat_z = share(summed(stat_y, st_y), st_z, "z", None)
    column.second()

    for copy in started[:early]:
        copy.wait_send()

    temperature = jnp.exp(jnp.broadcast_to(nef_ref[...], (XR, D)))
    for copy in (z1p, z1m, z2p, z2m):
        copy.wait_recv()
    full = own(0) + dx_near[0].astype(F32) + dx_near[1].astype(F32)
    full = full + dx_next[0].astype(F32) + dx_next[1].astype(F32)
    out_ref[0:XR, :] = temperature * full

    stats = jnp.sum(summed(stat_z, st_z), axis=1, keepdims=True) * (1.0 / PAIRS)
    lane_s = lax.broadcasted_iota(jnp.int32, (8, 128), 1)
    diagonal = lax.broadcasted_iota(jnp.int32, (8, 128), 0) == lane_s
    buckets = jnp.sum(jnp.where(diagonal, stats[0:8], 0.0), axis=0, keepdims=True)
    row_s = lax.broadcasted_iota(jnp.int32, (8, 128), 0)
    out = jnp.where(row_s == 0, buckets, 0.0)
    out = jnp.where(row_s == 1, stats[8:9], out)
    out = jnp.where(row_s == 2, stats[9:10], out)
    out = jnp.where(row_s == 3, -jnp.sum(stats[0:8], axis=0, keepdims=True), out)
    out_ref[XR + YR : XR + YR + 8, 0:128] = out

    mine = column.total()
    x2_done.wait_recv()
    mine = mine + x2_recv[...].astype(F32)
    out_ref[XR : XR + YR, :] = temperature[0:YR] * mine

    for copy in started[early:]:
        copy.wait_send()


COPIES = 192


def finish(packed, loss, gt, gw, bias, temp, penalty):
    gt[...] = packed[0:XR, :]
    gw[...] = packed[XR : XR + YR, :].reshape(YR, 1, D)
    penalty[...] = packed[XR + YR, 0:8]
    loss[...] = packed[XR + YR + 1, 0:1]
    temp[...] = packed[XR + YR + 2, 0:1]
    bias[...] = packed[XR + YR + 3, 0:1]


def local(timelines, windows, row_gap, col_gap, positive, nef, bias, deduction):
    vmem = pl.BlockSpec(memory_space=pltpu.VMEM)
    anywhere = pl.BlockSpec(memory_space=pltpu.HBM)
    shape = jax.ShapeDtypeStruct
    packed = pl.pallas_call(
        kernel,
        out_shape=shape((XR + YR + 8, D), F32),
        in_specs=[vmem] * 2 + [anywhere] * 6,
        out_specs=vmem,
        scratch_shapes=[
            pltpu.SMEM((8,), F32),
            pltpu.VMEM((1, XR), jnp.int32),
            pltpu.VMEM((1, XR), jnp.int32),
            pltpu.VMEM((1, YR), jnp.int32),
            pltpu.VMEM((NR, DE), BF16),
            pltpu.VMEM((NW, DE), BF16),
            pltpu.VMEM((NR, 128), BF16),
            pltpu.VMEM((NW, 128), BF16),
            pltpu.VMEM((NR, NW), F32),
            pltpu.VMEM((NR, NW), F32),
            pltpu.VMEM((NR, NW), BF16),
            pltpu.VMEM((NR, NW), BF16),
            pltpu.VMEM((NR, D), F32),
            pltpu.VMEM((HALF, D), F32),
            pltpu.VMEM((7, XR, D), BF16),
            pltpu.VMEM((2, XR, D), BF16),
            pltpu.VMEM((2, 16, D), BF16),
            pltpu.VMEM((2, XR, D), BF16),
            pltpu.VMEM((2, XR, D), F32),
            pltpu.VMEM((2, XR, D), BF16),
            pltpu.VMEM((NW, D), F32),
            pltpu.VMEM((2, 2, 64, D), BF16),
            pltpu.VMEM((2, 2, 64, D), BF16),
            pltpu.VMEM((2, 7, YR, D), BF16),
            pltpu.VMEM((2, 2, YR, D), BF16),
            pltpu.VMEM((2, 2, YR, 512), BF16),
            pltpu.VMEM((2, 2, YR, D), BF16),
            pltpu.VMEM((2, 2, YR, D), BF16),
            pltpu.VMEM((YR, D), BF16),
            pltpu.VMEM((YR, D), BF16),
            pltpu.VMEM((NX * 2, 16, 128), F32),
            pltpu.VMEM((NZ, 16, 128), F32),
            pltpu.VMEM((NY, 16, 128), F32),
            pltpu.SemaphoreType.DMA((6,)),
            pltpu.SemaphoreType.DMA((COPIES,)),
            pltpu.SemaphoreType.DMA((COPIES,)),
        ],
        compiler_params=pltpu.CompilerParams(
            collective_id=0, has_side_effects=True, vmem_limit_bytes=56 << 20
        ),
        name="loss_and_gradients",
    )(
        nef.reshape(1, 1), bias.reshape(1, 1), deduction, timelines, windows.reshape(YR, D),
        row_gap.reshape(1, XR), positive.reshape(1, XR), col_gap.reshape(1, YR),
    )
    return pl.pallas_call(
        finish,
        out_shape=(
            shape((1,), F32), shape((XR, D), F32), shape((YR, 1, D), F32),
            shape((1,), F32), shape((1,), F32), shape((8,), F32),
        ),
        in_specs=[vmem],
        out_specs=(vmem,) * 6,
        name="finish",
    )(packed)


def solution(mesh):
    return jax.shard_map(
        local,
        mesh=mesh,
        in_specs=(
            P(("row", "col"), None),
            P("row", "col", None),
            P(("row", "col")),
            P("row", "col"),
            P(("row", "col")),
            P(),
            P(),
            P(),
        ),
        out_specs=(P(), P(("row", "col"), None), P("row", "col", None), P(), P(), P()),
        check_vma=False,
    )
```
